32 devices in a mesh: ap: 8 (over y, x, core), pass: 4 (over z).
Axes of the slice: x: 2, y: 2, z: 4, core: 2. Of those that a mesh axis runs over, the one named last changes fastest.
Arguments:
- echo: bfloat16 [4, 64, 2, 3072], P('pass', 'ap'), may hold values from -6 to 6
- chirp: bfloat16 [2, 1024], replicated, may hold values from -0.125 to 0.125
- pair_swap: int32 [4, 6], P('pass'), may hold values from 0 to 1
- range_shift: int32 [4, 6, 2], P('pass'), may hold values from -16 to 16, as said below
- angle_shift: int32 [4, 6, 2, 2], P('pass'), may hold values from -3 to 3, as said below
- range_taps: float32 [6, 2, 8], replicated, may hold values from -2 to 2
- angle_taps: float32 [6, 2, 2, 8], replicated, may hold values from -2 to 2
- phase_rates: float32 [6, 2, 2, 2], replicated, may hold values from -3.140625 to 3.140625
- invert: float32 [2, 64, 32], replicated, may hold values from -2 to 2
- baseline_index: int32 [4], replicated, may hold values from 0 to 31
Outputs:
- tomogram: float32 [4, 64, 8, 4096], P('pass', None, 'ap')
The draws below stay inside these ranges and needn't reach their ends.
Inputs may be any that keep to these rules, and one draw needn't show every extreme that they name: `range_shift`: both 16 and -16 occur. `angle_shift`: both 3 and -3 occur.
All inputs are finite; a program needn't handle non-finite values.
Results may differ from the reference program's by a relative error of at most 0.0003.
Values sent between devices are 32-bit elements; how exact they have to be, the bound alone decides.
A program may use at most 64 MiB of HBM per device.

```python
import math
import jax
import jax.numpy as jnp
from jax import lax

NR = 2048
TAPS = 1024
HEIGHTS = 64
KT = 8
RMAX = 16
AMAX = 3
BASES = 32
NS = 3072
PULSES = 64
PASSES = 4
RW = 256
XLEV = 3
LEVELS = 6
RLEV = 6
N_AP = 8


def draw_extremes(key, layout, extreme):
    entries = math.prod(layout)
    values = jax.random.randint(key, (entries,), -extreme, extreme + 1, dtype=jnp.int32)
    shuffled = jax.random.permutation(jax.random.fold_in(key, 7), entries)
    values = values.at[shuffled[0]].set(extreme).at[shuffled[1]].set(-extreme)
    return values.reshape(layout)


def draw_range_shift(key, part):
    return draw_extremes(jax.random.fold_in(key, 11), (PASSES, RLEV, 2), RMAX)


def draw_angle_shift(key, part):
    return draw_extremes(jax.random.fold_in(key, 13), (PASSES, LEVELS, 2, 2), AMAX)


def place_ends(array, stream_key, smallest, high):
    dims = array.shape
    index_at = [jax.random.randint(jax.random.fold_in(stream_key, axis), (), 0, dims[axis]) for axis in range(len(dims))]
    array = array.at[tuple(index_at)].set(smallest)
    longest = dims.index(max(dims))
    index_at[longest] = (index_at[longest] + 1) % dims[longest]
    return array.at[tuple(index_at)].set(high)


def block_levels(own_key, shape, cuts, least, top_value):
    def one(axis_at, parts):
        heights = jax.random.uniform(jax.random.fold_in(jax.random.fold_in(own_key, 6), axis_at), (parts,), jnp.float32, least / len(cuts), top_value / len(cuts))
        return jnp.repeat(jnp.exp(heights), shape[axis_at] // parts).reshape((-1,) + (1,) * (len(shape) - axis_at - 1))

    factor_of = one(*cuts[0])
    for cut in cuts[1:]:
        factor_of = factor_of * one(*cut)
    return factor_of


def gaussian(stream_key, dims, scale, limit, cuts=(), held_as=jnp.bfloat16):
    array = scale * jax.random.normal(stream_key, dims, jnp.float32)
    if cuts:
        array = array * block_levels(stream_key, dims, cuts, -0.22, 0.18)
    return jnp.clip(array, -limit, limit).astype(held_as)


def setup_inputs(seed: int = 0) -> dict:
    key_list = jax.random.split(jax.random.key(seed), 11)
    echo = gaussian(key_list[0], (PASSES, PULSES, 2, NS), 1.0, 6.0, ((0, 4), (1, 8)))
    chirp = gaussian(key_list[1], (2, TAPS), (2 * TAPS) ** -0.5, 0.125)
    pair_swap = place_ends(jax.random.randint(key_list[2], (PASSES, LEVELS), 0, 2), jax.random.fold_in(key_list[2], 1), 0, 1).astype(jnp.int32)
    range_shift = draw_range_shift(jax.random.fold_in(key_list[10], 71), 0)
    angle_shift = draw_angle_shift(jax.random.fold_in(key_list[10], 71), 0)
    range_taps = gaussian(key_list[5], (RLEV, 2, KT), KT ** -0.5, 2.0, (), jnp.float32)
    angle_taps = gaussian(key_list[6], (LEVELS, 2, 2, KT), KT ** -0.5, 2.0, (), jnp.float32)
    phase_rates = jnp.clip(jax.random.uniform(key_list[7], (LEVELS, 2, 2, 2), jnp.float32, -3.140625, 3.140625), -3.140625, 3.140625)
    invert = gaussian(key_list[8], (2, HEIGHTS, BASES), (2 * PASSES) ** -0.5, 2.0, (), jnp.float32)
    baseline_index = place_ends(jax.random.randint(key_list[9], (PASSES,), 0, BASES), jax.random.fold_in(key_list[9], 1), 0, BASES - 1).astype(jnp.int32)
    return dict(echo=echo, chirp=chirp, pair_swap=pair_swap, range_shift=range_shift, angle_shift=angle_shift, range_taps=range_taps, angle_taps=angle_taps, phase_rates=phase_rates, invert=invert, baseline_index=baseline_index)


SQRT_HALF = math.sqrt(0.5)

def interp(values, tap_row, offset, along, margin, fill_mode):
    length = values.shape[along]
    widths = [(0, 0)] * values.ndim
    widths[along] = (margin, margin)
    padded = jnp.pad(values, widths, mode=fill_mode)
    summed = jnp.zeros_like(values)
    for position in range(tap_row.shape[0]):
        begin_at = margin + position - (KT // 2 - 1) + offset
        summed = summed + tap_row[position] * lax.dynamic_slice_in_dim(padded, begin_at, length, along)
    return summed

def merge_pair(first, second, section_index, flip, range_row, angle_row, range_taps, angle_taps, phase_rates, r_frac, j_grid, beam_axis, range_axis, trim):
    beams = first.shape[beam_axis]
    prepared = []
    for c, child in enumerate((first, second)):
        role_index = (c + flip) % 2
        child = interp(child, range_taps[section_index, role_index], range_row[section_index, role_index], range_axis, RMAX + KT, 'constant')
        if trim > 0:
            child = lax.slice_in_dim(child, trim, child.shape[range_axis] - trim, axis=range_axis)
        prepared.append((child, role_index))
    results = []
    for h in range(2):
        terms = []
        for child, role_index in prepared:
            steered = interp(child, angle_taps[section_index, role_index, h], angle_row[section_index, role_index, h], beam_axis, AMAX + KT, 'edge')
            rates = phase_rates[section_index, role_index, h]
            phase = 8.0 * (rates[0] * r_frac + rates[1] * ((2.0 * j_grid + h) / (2.0 * beams)))
            cosine = jnp.cos(phase)
            sine = jnp.sin(phase)
            terms.append(jnp.stack([cosine * steered[0] - sine * steered[1], sine * steered[0] + cosine * steered[1]], 0))
        results.append((terms[0] + terms[1]) * SQRT_HALF)
    stacked = jnp.stack(results, axis=beam_axis + 1)
    new_shape = list(results[0].shape)
    new_shape[beam_axis] = 2 * beams
    return stacked.reshape(new_shape)

def reference(echo, chirp, pair_swap, range_shift, angle_shift, range_taps, angle_taps, phase_rates, invert, baseline_index):
    window = jnp.arange(NS)[:, None] - jnp.arange(NR)[None, :]
    inside = (window >= 0) & (window < TAPS)
    clipped = jnp.clip(window, 0, TAPS - 1)
    chirp_wide = chirp.astype(jnp.float32)
    real_kernel = jnp.where(inside, chirp_wide[0][clipped], 0.0)
    imag_kernel = jnp.where(inside, chirp_wide[1][clipped], 0.0)
    highest = lax.Precision.HIGHEST

    def one_pass(inputs):
        echo_pass, swap_row, range_row, angle_row = inputs
        real_echo = echo_pass[:, 0].astype(jnp.float32)
        imag_echo = echo_pass[:, 1].astype(jnp.float32)
        real_out = jnp.dot(real_echo, real_kernel, precision=highest, preferred_element_type=jnp.float32) + jnp.dot(imag_echo, imag_kernel, precision=highest, preferred_element_type=jnp.float32)
        imag_out = jnp.dot(imag_echo, real_kernel, precision=highest, preferred_element_type=jnp.float32) - jnp.dot(real_echo, imag_kernel, precision=highest, preferred_element_type=jnp.float32)
        image = jnp.stack([real_out, imag_out], 0).reshape(2, PULSES, 1, NR)
        r_frac = (jnp.arange(NR, dtype=jnp.float32) / NR)[None, :]
        for section_index in range(LEVELS):
            groups = image.shape[1]
            beams = image.shape[2]
            pairs = image.reshape(2, groups // 2, 2, beams, NR)
            j_grid = jnp.arange(beams, dtype=jnp.float32)[:, None]
            image = merge_pair(pairs[:, :, 0], pairs[:, :, 1], section_index, swap_row[section_index], range_row, angle_row, range_taps, angle_taps, phase_rates, r_frac, j_grid, 2, 3, 0)
        return image[:, 0]
    images = lax.map(one_pass, (echo, pair_swap, range_shift, angle_shift))
    steer = invert[:, :, baseline_index]

    def one_block(block_index):
        reversed_index = jnp.zeros((), jnp.int32)
        for digit in range(XLEV):
            reversed_index = reversed_index + block_index // 2 ** digit % 2 * 2 ** (XLEV - 1 - digit)
        piece = lax.dynamic_slice_in_dim(images, (reversed_index * RW).astype(jnp.int32), RW, 3)
        real_sum = jnp.einsum('hp,pqr->hrq', steer[0], piece[:, 0], precision=highest) - jnp.einsum('hp,pqr->hrq', steer[1], piece[:, 1], precision=highest)
        imag_sum = jnp.einsum('hp,pqr->hrq', steer[1], piece[:, 0], precision=highest) + jnp.einsum('hp,pqr->hrq', steer[0], piece[:, 1], precision=highest)
        return real_sum * real_sum + imag_sum * imag_sum
    blocks = lax.map(one_block, jnp.arange(N_AP, dtype=jnp.int32))
    per_pass = PULSES // PASSES
    split = blocks.reshape(N_AP, HEIGHTS, RW, PASSES, per_pass)
    return jnp.transpose(split, (3, 1, 0, 2, 4)).reshape(PASSES, HEIGHTS, N_AP, RW * per_pass)
```

```python
import functools
import math

import jax
import jax.numpy as jnp
from jax import lax
from jax.experimental import pallas as pl
from jax.experimental.pallas import tpu as pltpu
from jax.sharding import PartitionSpec as P

RMAX = 16
PAD = 24
F32 = jnp.float32
BF16 = jnp.bfloat16
MESH = pl.DeviceIdType.MESH
LANES = 128


def up(value, unit):
    return -(-value // unit) * unit


def lane_iota(rows, lanes):
    return lax.broadcasted_iota(jnp.int32, (rows, lanes), 1)


def row_iota(rows, lanes):
    return lax.broadcasted_iota(jnp.int32, (rows, lanes), 0)


def sincos(theta):
    turns = jnp.floor(theta * (2.0 / math.pi) + 0.5)
    rest = theta - turns * 1.5703125
    rest = rest - turns * 4.837512969970703125e-4
    rest = rest - turns * 7.549789948768648e-8
    sq = rest * rest
    sine = rest + rest * sq * (
        -1.6666654611e-1 + sq * (8.3321608736e-3 + sq * -1.9515295891e-4)
    )
    cosine = 1.0 - 0.5 * sq + sq * sq * (
        4.166664568298827e-2 + sq * (-1.388731625493765e-3 + sq * 2.443315711809948e-5)
    )
    quadrant = turns.astype(jnp.int32) & 3
    odd = (quadrant & 1) == 1
    sin_out = jnp.where(odd, cosine, sine)
    cos_out = jnp.where(odd, sine, cosine)
    sin_out = jnp.where(quadrant >= 2, -sin_out, sin_out)
    cos_out = jnp.where((quadrant == 1) | (quadrant == 2), -cos_out, cos_out)
    return sin_out, cos_out


def take(ref, begin, rows, stride=None):
    where = pl.ds(begin, rows) if stride is None else pl.ds(begin, rows, stride=stride)
    return jnp.concatenate([ref[k, where, :] for k in range(ref.shape[0])], 1)


def put(ref, begin, value):
    for k in range(ref.shape[0]):
        ref[k, begin : begin + value.shape[0]] = value[:, k * LANES : (k + 1) * LANES]


def split(value):
    high = value.astype(BF16)
    low = (value - high.astype(F32)).astype(BF16)
    return high, low


def roles(swap_ref, level):
    swap = swap_ref[0, level]
    return [swap, 1 - swap]


def beam_matrix(level, beams, lanes, role, angle_shift, angle_taps):
    out_lane = lane_iota(8, lanes)[:1]
    q = out_lane & (2 * beams - 1)
    h_odd = (q & 1) == 1
    j_out = q >> 1
    core_rows = max(8, beams)
    j_in = row_iota(core_rows, lanes) & (beams - 1)
    in_row = row_iota(lanes, lanes)
    out_col = lane_iota(lanes, lanes)
    log_beams = beams.bit_length() - 1
    group_in = in_row >> (log_beams + 1)
    part_in = (in_row >> log_beams) & 1
    group_out = out_col >> (log_beams + 2)
    part_out = (out_col >> (log_beams + 1)) & 1
    same_part = part_in == part_out
    plain, turned = [], []
    for c in range(2):
        e = role[c]
        taps_count = angle_taps.shape[3]
        offset = jnp.where(
            h_odd, angle_shift[0, e, 1, level], angle_shift[0, e, 0, level]
        ) - (taps_count // 2 - 1)
        core = jnp.zeros((core_rows, lanes), F32)
        for u in range(taps_count):
            source = jnp.clip(j_out + offset + u, 0, beams - 1)
            weight = jnp.where(
                h_odd, angle_taps[level, e, 1, u], angle_taps[level, e, 0, u]
            ) * math.sqrt(0.5)
            core = core + jnp.where(j_in == source, weight, 0.0)
        full = jnp.concatenate([core] * (lanes // core_rows), 0)
        full = jnp.where(group_in == 2 * group_out + c, full, 0.0)
        plain.append(jnp.where(same_part, full, 0.0))
        turned.append(
            jnp.where(same_part, 0.0, jnp.where(part_out == 0, -full, full))
        )
    high, low = split(jnp.concatenate(plain + turned, 1))
    return jnp.concatenate([high, high, low], 0)


def phase_tables(level, beams, lanes, role, rates, origin, cells, count):
    q = lane_iota(8, lanes)[:1] & (2 * beams - 1)
    h_odd = (q & 1) == 1
    beam_at = q.astype(F32) * (1.0 / (2 * beams))
    row = row_iota(8, lanes)
    tiles = count // 8
    doublings = max(tiles - 1, 1).bit_length()
    tables = []
    for c in range(2):
        e = role[c]
        slope = jnp.where(h_odd, rates[e, 1, 0, level], rates[e, 0, 0, level]) * (8.0 / cells)
        tilt = jnp.where(h_odd, rates[e, 1, 1, level], rates[e, 0, 1, level]) * 8.0
        first = slope * (origin + row).astype(F32) + tilt * beam_at
        steps = slope * (8 << row).astype(F32)
        sines, cosines = sincos(jnp.concatenate([first, steps], 0))
        sin_tiles, cos_tiles = [sines[:8]], [cosines[:8]]
        for m in range(doublings):
            s_step, c_step = sines[8 + m : 9 + m], cosines[8 + m : 9 + m]
            for a in range(1 << m):
                if len(sin_tiles) < tiles:
                    s_old, c_old = sin_tiles[a], cos_tiles[a]
                    sin_tiles.append(s_old * c_step + c_old * s_step)
                    cos_tiles.append(c_old * c_step - s_old * s_step)
        tables.append((jnp.concatenate(cos_tiles, 0), jnp.concatenate(sin_tiles, 0)))
    return tables


def merge(level, beams, lo, hi, src, z_ref, params, origin, cells):
    swap_ref, range_shift, angle_shift, range_taps, angle_taps, rates = params
    lanes = src.shape[0] * LANES
    rows = hi - lo
    role = roles(swap_ref, level)
    child = (lane_iota(8, lanes)[:1] >> beams.bit_length()) & 1
    taps_count = range_taps.shape[2]
    o = taps_count // 2 - 1
    starts = [PAD + lo - o + range_shift[0, e, level] for e in role]
    aligned = jnp.where(
        child == 0, take(src, starts[0], rows + 8), take(src, starts[1], rows + 8)
    )
    put(z_ref, 0, aligned)
    ranged = jnp.zeros((rows, lanes), F32)
    for t in range(taps_count):
        weight = jnp.where(
            child == 0, range_taps[level, role[0], t], range_taps[level, role[1], t]
        )
        ranged = ranged + weight * take(z_ref, t, rows)
    high, low = split(ranged)
    weights = beam_matrix(level, beams, lanes, role, angle_shift, angle_taps)
    product = jnp.dot(
        jnp.concatenate([high, low, high], 1), weights, preferred_element_type=F32
    )
    (cos0, sin0), (cos1, sin1) = phase_tables(
        level, beams, lanes, role, rates, origin + lo, cells, rows
    )
    return (
        cos0 * product[:, :lanes]
        + cos1 * product[:, lanes : 2 * lanes]
        + sin0 * product[:, 2 * lanes : 3 * lanes]
        + sin1 * product[:, 3 * lanes :]
    )


def image_kernel(
    sizes,
    echo,
    chirp,
    swap_ref,
    range_shift,
    angle_shift,
    range_taps,
    angle_taps,
    rates,
    out,
    echo_rows,
    chirp_rows,
    image_a,
    image_b,
    z_ref,
    send_ap,
    recv_ap,
    send_pass,
    send_sem,
    recv_sem,
    send_sem2,
    recv_sem2,
):
    n, passes, pulses, cells, levels = sizes
    lanes = n * 2 * pulses
    taps_count = chirp.shape[1]
    samples = echo.shape[3]
    block = cells // n
    reach = RMAX + range_taps.shape[2] // 2
    local = pulses.bit_length() - 1
    cross = levels - local
    wide = up(block + 2 * reach * cross, LANES)
    halo = (wide - block) // 2
    rim = up(reach * local, 64)
    window = wide + 2 * rim
    start = halo + rim
    me = lax.axis_index("ap")
    my_pass = lax.axis_index("pass")
    params = (swap_ref, range_shift, angle_shift, range_taps, angle_taps, rates)

    def rev(index):
        total = 0
        for digit in range(cross):
            total = total + (index // 2**digit) % 2 * 2 ** (cross - 1 - digit)
        return total

    barrier = pltpu.get_barrier_semaphore()
    for i in range(1, n):
        pl.semaphore_signal(
            barrier, inc=1, device_id=(lax.rem(me + i, n), my_pass), device_id_type=MESH
        )
    for i in range(1, passes):
        pl.semaphore_signal(
            barrier, inc=1, device_id=(me, lax.rem(my_pass + i, passes)), device_id_type=MESH
        )

    depth = up(block + taps_count - 1, LANES)
    for pulse in range(pulses):
        echo_rows[2 * pulse : 2 * pulse + 2, :samples] = echo[0, pulse].astype(F32)
    need = block * (n - 1) + depth
    if need > samples:
        echo_rows[:, samples:] = jnp.zeros((2 * pulses, echo_rows.shape[1] - samples), F32)
    echo_cat = jnp.concatenate(
        [echo_rows[:, k * block : k * block + depth].astype(BF16) for k in range(n)], 0
    )
    taps = chirp[...].astype(F32)
    sub = row_iota(8, depth)
    for part in range(2):
        wide_row = jnp.concatenate(
            [
                jnp.broadcast_to(taps[part : part + 1], (8, taps_count)),
                jnp.zeros((8, depth - taps_count), F32),
            ],
            1,
        )
        base = wide_row
        for s in range(1, 8):
            base = jnp.where(sub == s, pltpu.roll(wide_row, s, 1), base)
        for a in range(0, min(block, LANES), 16):
            pair = [base if a == 0 else pltpu.roll(base, a, 1), pltpu.roll(base, a + 8, 1)]
            rows16 = jnp.concatenate(pair, 0).astype(BF16)
            for b in range(max(block // LANES, 1)):
                if b:
                    rows16 = jnp.concatenate([rows16[:, -LANES:], rows16[:, :-LANES]], 1)
                at = part * block + b * LANES + a
                chirp_rows[at : at + 16, :] = rows16
    product = lax.dot_general(
        chirp_rows[...], echo_cat, (((1,), (1,)), ((), ())), preferred_element_type=F32
    )
    crossed = product[block:]
    odd = (lane_iota(8, lanes)[:1] & 1) == 1
    compressed = product[:block] + jnp.where(
        odd, -pltpu.roll(crossed, 1, 1), pltpu.roll(crossed, lanes - 1, 1)
    )

    per = 2 * pulses
    lane_block = lane_iota(8, lanes)[:1] >> (per.bit_length() - 1)

    def pieces(lo, hi):
        at = lo
        while at < hi:
            q = (at - start) // block
            end = min(hi, start + (q + 1) * block)
            yield at, end, q
            at = end

    def keep(q):
        return (lane_block + q >= 0) & (lane_block + q < n)

    blank = jnp.zeros((PAD + 24, lanes), F32)
    put(image_a, 0, blank[:PAD])
    put(image_b, 0, blank)
    put(image_a, PAD + window, blank[:PAD])
    put(image_b, PAD + window - 24, blank)
    for at, end, q in pieces(0, window):
        from_row = at - start - q * block
        piece = compressed[from_row : from_row + end - at]
        if q:
            piece = jnp.where(keep(q), pltpu.roll(piece, (-q * per) % lanes, 1), 0.0)
        put(image_a, PAD + at, piece)

    origin = lane_block * block - start
    src, dst = image_a, image_b
    for level in range(local):
        margin = (level + 1) * reach // 8 * 8 if level + 1 < local else rim
        merged = merge(
            level, 2**level, margin, window - margin, src, z_ref, params, origin, cells
        )
        masked = []
        for at, end, q in pieces(margin, window - margin):
            piece = merged[at - margin : end - margin]
            masked.append(jnp.where(keep(q), piece, 0.0) if q else piece)
        merged = jnp.concatenate(masked, 0)
        if level + 1 < local:
            put(dst, PAD + margin, merged)
            src, dst = dst, src
    send_ap[...] = merged.T.reshape(n, per, wide)

    pl.semaphore_wait(barrier, n - 1 + passes - 1)
    copies = []
    for i in range(1, n):
        to = lax.rem(me + i, n)
        copy = pltpu.make_async_remote_copy(
            src_ref=send_ap.at[rev(to)],
            dst_ref=recv_ap.at[me],
            send_sem=send_sem.at[i],
            recv_sem=recv_sem.at[i],
            device_id=(to, my_pass),
            device_id_type=MESH,
        )
        copy.start()
        copies.append(copy)
    recv_ap[me] = send_ap[rev(me)]
    for copy in copies:
        copy.wait()
    put(image_a, PAD, recv_ap[...].reshape(lanes, wide).T)
    put(image_a, PAD + wide, blank[:PAD])
    put(image_b, PAD + wide - 24, blank)

    origin = rev(me) * block - halo
    src, dst = image_a, image_b
    for digit in range(cross):
        level = local + digit
        last = digit + 1 == cross
        margin = halo if last else (digit + 1) * reach // 8 * 8
        merged = merge(
            level, 2**level, margin, wide - margin, src, z_ref, params, origin, cells
        )
        if not last:
            at = origin + margin + row_iota(wide - 2 * margin, lanes)
            merged = jnp.where((at >= 0) & (at < cells), merged, 0.0)
        put(dst, PAD + margin, merged)
        src, dst = dst, src

    beams = 2**levels
    share = beams // passes
    spread = LANES // share
    count = block // spread
    group = lane_iota(8, LANES)[:1] >> (share.bit_length() - 1)
    rows = [take(src, PAD + halo + s, count, spread) for s in range(spread)]
    for b in range(passes):
        for c in range(2):
            lane = c * beams + b * share
            base, inner = lane // LANES * LANES, lane % LANES
            gathered = None
            for s in range(spread):
                moved = pltpu.roll(
                    rows[s][:, base : base + LANES], (s * share - inner) % LANES, 1
                )
                gathered = moved if s == 0 else jnp.where(group == s, moved, gathered)
            send_pass[b, c * count : (c + 1) * count] = gathered
    copies = []
    for i in range(1, passes):
        to = lax.rem(my_pass + i, passes)
        copy = pltpu.make_async_remote_copy(
            src_ref=send_pass.at[to],
            dst_ref=out.at[my_pass],
            send_sem=send_sem2.at[i],
            recv_sem=recv_sem2.at[i],
            device_id=(me, to),
            device_id_type=MESH,
        )
        copy.start()
        copies.append(copy)
    out[my_pass] = send_pass[my_pass]
    for copy in copies:
        copy.wait()


def power_kernel(passes, count, data, invert, baseline, out):
    bases, heights = invert.shape[1], invert.shape[2]
    real, imag = invert[0], invert[1]
    table = jnp.concatenate(
        [jnp.concatenate([real, imag], 1), jnp.concatenate([-imag, real], 1)], 0
    ).T
    table_high, table_low = split(table)
    row = row_iota(2 * bases, 2 * passes)
    column = lane_iota(2 * bases, 2 * passes)
    chosen = jnp.zeros((2 * bases, 2 * passes), F32)
    for p in range(passes):
        for c in range(2):
            hit = (column == 2 * p + c) & (row == c * bases + baseline[p])
            chosen = jnp.where(hit, 1.0, chosen)
    chosen = chosen.astype(BF16)
    mixer_high = jnp.dot(table_high, chosen, preferred_element_type=F32).astype(BF16)
    mixer_low = jnp.dot(table_low, chosen, preferred_element_type=F32).astype(BF16)
    mixer = jnp.concatenate([mixer_high, mixer_high, mixer_low], 1)
    chunk = min(count, 8)
    for a0 in range(0, count, chunk):
        values = jnp.concatenate(
            [data[pl.ds(a, 2 * passes, stride=count), :] for a in range(a0, a0 + chunk)], 1
        )
        high = values.astype(BF16).astype(F32)
        low = values - high
        stack = jnp.concatenate([high, low, high], 0).astype(BF16)
        tomo = jnp.dot(mixer, stack, preferred_element_type=F32)
        power = tomo[:heights] * tomo[:heights] + tomo[heights:] * tomo[heights:]
        for a in range(chunk):
            out[pl.ds(a0 + a, heights, stride=count), :] = power[:, a * LANES : (a + 1) * LANES]


def body(
    mesh_shape,
    echo,
    chirp,
    pair_swap,
    range_shift,
    angle_shift,
    range_taps,
    angle_taps,
    phase_rates,
    invert,
    baseline_index,
):
    n, passes = mesh_shape["ap"], mesh_shape["pass"]
    pulses, samples = echo.shape[1], echo.shape[3]
    levels = range_taps.shape[0]
    taps_count = chirp.shape[1]
    cells = samples - taps_count
    block = cells // n
    beams = 2**levels
    share = beams // passes
    heights = invert.shape[1]
    count = block * share // LANES
    lanes = n * 2 * pulses
    reach = RMAX + range_taps.shape[2] // 2
    local = pulses.bit_length() - 1
    wide = up(block + 2 * reach * (levels - local), LANES)
    window = wide + 2 * up(reach * local, 64)
    depth = up(block + taps_count - 1, LANES)
    vmem = pl.BlockSpec(memory_space=pltpu.VMEM)
    smem = pl.BlockSpec(memory_space=pltpu.SMEM)
    stacks = pl.pallas_call(
        functools.partial(image_kernel, (n, passes, pulses, cells, levels)),
        out_shape=jax.ShapeDtypeStruct((passes, 2 * count, LANES), F32),
        in_specs=[vmem] * 2 + [smem] * 6,
        out_specs=vmem,
        scratch_shapes=[
            pltpu.VMEM((2 * pulses, up(max(samples, block * (n - 1) + depth), LANES)), F32),
            pltpu.VMEM((2 * block, depth), BF16),
            pltpu.VMEM((lanes // LANES, window + 2 * PAD, LANES), F32),
            pltpu.VMEM((lanes // LANES, window + 2 * PAD, LANES), F32),
            pltpu.VMEM((lanes // LANES, window, LANES), F32),
            pltpu.VMEM((n, 2 * pulses, wide), F32),
            pltpu.VMEM((n, 2 * pulses, wide), F32),
            pltpu.VMEM((passes, 2 * count, LANES), F32),
            pltpu.SemaphoreType.DMA((n,)),
            pltpu.SemaphoreType.DMA((n,)),
            pltpu.SemaphoreType.DMA((passes,)),
            pltpu.SemaphoreType.DMA((passes,)),
        ],
        compiler_params=pltpu.CompilerParams(
            collective_id=0, has_side_effects=True, vmem_limit_bytes=48 * 2**20
        ),
        name="image",
    )(
        echo,
        chirp,
        pair_swap,
        jnp.transpose(range_shift, (0, 2, 1)),
        jnp.transpose(angle_shift, (0, 2, 3, 1)),
        range_taps,
        angle_taps,
        jnp.transpose(phase_rates, (1, 2, 3, 0)),
    )
    power = pl.pallas_call(
        functools.partial(power_kernel, passes, count),
        out_shape=jax.ShapeDtypeStruct((heights * count, LANES), F32),
        in_specs=[vmem, vmem, smem],
        out_specs=vmem,
        compiler_params=pltpu.CompilerParams(vmem_limit_bytes=32 * 2**20),
        name="power",
    )(
        stacks.reshape(passes * 2 * count, LANES),
        jnp.transpose(invert, (0, 2, 1)),
        baseline_index,
    )
    return power.reshape(1, heights, 1, block * share)


def solution(mesh):
    return jax.shard_map(
        functools.partial(body, dict(mesh.shape)),
        mesh=mesh,
        in_specs=(
            P("pass", "ap", None, None),
            P(),
            P("pass", None),
            P("pass", None, None),
            P("pass", None, None, None),
            P(),
            P(),
            P(),
            P(),
            P(),
        ),
        out_specs=P("pass", None, "ap", None),
        check_vma=False,
    )
```

```python
import functools
import math

import jax
import jax.numpy as jnp
from jax import lax
from jax.experimental import pallas as pl
from jax.experimental.pallas import tpu as pltpu
from jax.sharding import PartitionSpec as P

RMAX = 16
PAD = 24
F32 = jnp.float32
BF16 = jnp.bfloat16
MESH = pl.DeviceIdType.MESH
LANES = 128


def up(value, unit):
    return -(-value // unit) * unit


def lane_iota(rows, lanes):
    return lax.broadcasted_iota(jnp.int32, (rows, lanes), 1)


def row_iota(rows, lanes):
    return lax.broadcasted_iota(jnp.int32, (rows, lanes), 0)


def sincos(theta):
    turns = jnp.floor(theta * (2.0 / math.pi) + 0.5)
    rest = theta - turns * 1.5703125
    rest = rest - turns * 4.837512969970703125e-4
    rest = rest - turns * 7.549789948768648e-8
    sq = rest * rest
    sine = rest + rest * sq * (
        -1.6666654611e-1 + sq * (8.3321608736e-3 + sq * -1.9515295891e-4)
    )
    cosine = 1.0 - 0.5 * sq + sq * sq * (
        4.166664568298827e-2 + sq * (-1.388731625493765e-3 + sq * 2.443315711809948e-5)
    )
    quadrant = turns.astype(jnp.int32) & 3
    odd = (quadrant & 1) == 1
    sin_out = jnp.where(odd, cosine, sine)
    cos_out = jnp.where(odd, sine, cosine)
    sin_out = jnp.where(quadrant >= 2, -sin_out, sin_out)
    cos_out = jnp.where((quadrant == 1) | (quadrant == 2), -cos_out, cos_out)
    return sin_out, cos_out


def take(ref, begin, rows, stride=None):
    where = pl.ds(begin, rows) if stride is None else pl.ds(begin, rows, stride=stride)
    return jnp.concatenate([ref[k, where, :] for k in range(ref.shape[0])], 1)


def put(ref, begin, value):
    for k in range(ref.shape[0]):
        ref[k, begin : begin + value.shape[0]] = value[:, k * LANES : (k + 1) * LANES]


def split(value):
    high = value.astype(BF16)
    low = (value - high.astype(F32)).astype(BF16)
    return high, low


def roles(swap_ref, level):
    swap = swap_ref[0, level]
    return [swap, 1 - swap]


def prepare(level, beams, origin, tiles, cells, params, w_ref, table_ref):
    swap_ref, _, angle_shift, _, angle_taps, rates = params
    lanes = w_ref.shape[2] // 4
    role = roles(swap_ref, level)
    taps_count = angle_taps.shape[3]
    q = lane_iota(8, lanes)[:1] & (2 * beams - 1)
    h_odd = (q & 1) == 1
    j_out = q >> 1
    log_beams = beams.bit_length() - 1
    part_out = (lane_iota(16, lanes) >> (log_beams + 1)) & 1
    group_out = lane_iota(16, lanes) >> (log_beams + 2)
    core_rows = max(16, beams)
    j_in = row_iota(core_rows, lanes) & (beams - 1)
    cores = []
    for e in role:
        offset = jnp.where(
            h_odd, angle_shift[0, e, 1, level], angle_shift[0, e, 0, level]
        ) - (taps_count // 2 - 1)
        core = jnp.zeros((core_rows, lanes), F32)
        for u in range(taps_count):
            source = jnp.clip(j_out + offset + u, 0, beams - 1)
            weight = jnp.where(
                h_odd, angle_taps[level, e, 1, u], angle_taps[level, e, 0, u]
            ) * math.sqrt(0.5)
            core = core + jnp.where(j_in == source, weight, 0.0)
        cores.append(core)
    for at in range(0, lanes, 16):
        in_row = at + row_iota(16, lanes)
        group_in = in_row >> (log_beams + 1)
        same_part = ((in_row >> log_beams) & 1) == part_out
        for c in range(2):
            core = cores[c][at % core_rows : at % core_rows + 16]
            full = jnp.where(group_in == 2 * group_out + c, core, 0.0)
            plain = jnp.where(same_part, full, 0.0)
            turned = jnp.where(same_part, 0.0, jnp.where(part_out == 0, -full, full))
            for place, value in ((c, plain), (2 + c, turned)):
                high, low = split(value)
                columns = slice(place * lanes, (place + 1) * lanes)
                w_ref[level, at : at + 16, columns] = high
                w_ref[level, lanes + at : lanes + at + 16, columns] = high
                w_ref[level, 2 * lanes + at : 2 * lanes + at + 16, columns] = low

    beam_at = q.astype(F32) * (1.0 / (2 * beams))
    row = row_iota(8, lanes)
    groups = -(-tiles // 8)
    for c, e in enumerate(role):
        slope = jnp.where(h_odd, rates[e, 1, 0, level], rates[e, 0, 0, level]) * (8.0 / cells)
        tilt = jnp.where(h_odd, rates[e, 1, 1, level], rates[e, 0, 1, level]) * 8.0
        first = slope * (origin + row).astype(F32) + tilt * beam_at
        along = slope * (8 * row).astype(F32)
        steps = slope * (64 << row).astype(F32)
        sines, cosines = sincos(jnp.concatenate([first, along, steps], 0))
        table_ref[level, c, 0, :8] = cosines[:8]
        table_ref[level, c, 1, :8] = sines[:8]
        held = [(cosines[8:16], sines[8:16])]
        m = 0
        while len(held) < groups:
            s_step, c_step = sines[16 + m : 17 + m], cosines[16 + m : 17 + m]
            for c_old, s_old in held[: groups - len(held)]:
                held.append((c_old * c_step - s_old * s_step, s_old * c_step + c_old * s_step))
            m += 1
        for k, (cosine, sine) in enumerate(held):
            table_ref[level, c, 0, 8 + 8 * k : 16 + 8 * k] = cosine
            table_ref[level, c, 1, 8 + 8 * k : 16 + 8 * k] = sine


def merge(level, beams, lo, hi, src, dst, valid, params, z_ref, x_ref, p_ref, w_ref, table_ref):
    swap_ref, range_shift, _, range_taps, _, _ = params
    lanes = src.shape[0] * LANES
    rows = hi - lo
    role = roles(swap_ref, level)
    child = (lane_iota(8, lanes)[:1] >> beams.bit_length()) & 1
    first = child == 0
    taps_count = range_taps.shape[2]
    o = taps_count // 2 - 1
    starts = [PAD + lo - o + range_shift[0, e, level] for e in role]
    for at in range(0, rows + 8, 64):
        n = min(64, rows + 8 - at)
        put(z_ref, at, jnp.where(first, take(src, starts[0] + at, n), take(src, starts[1] + at, n)))
    weights = [
        jnp.where(first, range_taps[level, role[0], t], range_taps[level, role[1], t])
        for t in range(taps_count)
    ]
    for at in range(0, rows, 32):
        n = min(32, rows - at)
        ranged = weights[0] * take(z_ref, at, n)
        for t in range(1, taps_count):
            ranged = ranged + weights[t] * take(z_ref, at + t, n)
        high, low = split(ranged)
        x_ref[at : at + n, :lanes] = high
        x_ref[at : at + n, lanes : 2 * lanes] = low
        x_ref[at : at + n, 2 * lanes :] = high
    p_ref[:rows] = jnp.dot(x_ref[:rows], w_ref[level], preferred_element_type=F32)
    base = [(table_ref[level, c, 0, :8], table_ref[level, c, 1, :8]) for c in range(2)]
    for a in range(rows // 8):
        total = None
        for c in range(2):
            c_step = table_ref[level, c, 0, 8 + a : 9 + a]
            s_step = table_ref[level, c, 1, 8 + a : 9 + a]
            c_base, s_base = base[c]
            cosine = c_base * c_step - s_base * s_step
            sine = s_base * c_step + c_base * s_step
            plain = p_ref[8 * a : 8 * a + 8, c * lanes : (c + 1) * lanes]
            turned = p_ref[8 * a : 8 * a + 8, (2 + c) * lanes : (3 + c) * lanes]
            term = cosine * plain + sine * turned
            total = term if c == 0 else total + term
        at = lo + 8 * a
        if valid is not None:
            origin, block, halo, cells = valid
            if at < halo or at >= halo + block:
                cell = origin + at + row_iota(8, lanes)
                total = jnp.where((cell >= 0) & (cell < cells), total, 0.0)
        put(dst, PAD + at, total)


def image_kernel(
    sizes,
    echo_in,
    chirp_in,
    swap_in,
    range_shift_in,
    angle_shift_in,
    range_taps_in,
    angle_taps_in,
    rates_in,
    invert_in,
    baseline_in,
    out,
    mixer,
    echo,
    chirp,
    swap_ref,
    range_shift,
    angle_shift,
    range_taps,
    angle_taps,
    rates,
    invert,
    baseline,
    echo_rows,
    chirp_rows,
    image_a,
    image_b,
    z_ref,
    x_ref,
    p_ref,
    w_ref,
    table_ref,
    send_ap,
    recv_ap,
    send_pass,
    in_sem,
    send_sem,
    recv_sem,
    send_sem2,
    recv_sem2,
):
    n, passes, pulses, cells, levels = sizes
    lanes = n * 2 * pulses
    taps_count = chirp.shape[1]
    samples = echo.shape[3]
    block = cells // n
    reach = RMAX + range_taps.shape[2] // 2
    local = pulses.bit_length() - 1
    cross = levels - local
    wide = up(block + 2 * reach * cross, LANES)
    halo = (wide - block) // 2
    me = lax.axis_index("ap")
    my_pass = lax.axis_index("pass")
    params = (swap_ref, range_shift, angle_shift, range_taps, angle_taps, rates)

    def rev(index):
        total = 0
        for digit in range(cross):
            total = total + (index // 2**digit) % 2 * 2 ** (cross - 1 - digit)
        return total

    pairs = [
        (swap_in, swap_ref),
        (angle_shift_in, angle_shift),
        (angle_taps_in, angle_taps),
        (rates_in, rates),
        (range_shift_in, range_shift),
        (range_taps_in, range_taps),
        (baseline_in, baseline),
        (chirp_in, chirp),
        (echo_in, echo),
        (invert_in, invert),
    ]
    fetches = [
        pltpu.make_async_copy(there, here, in_sem.at[i]) for i, (there, here) in enumerate(pairs)
    ]
    for fetch in fetches:
        fetch.start()

    barrier = pltpu.get_barrier_semaphore()
    for i in range(1, n):
        pl.semaphore_signal(
            barrier, inc=1, device_id=(lax.rem(me + i, n), my_pass), device_id_type=MESH
        )
    for i in range(1, passes):
        pl.semaphore_signal(
            barrier, inc=1, device_id=(me, lax.rem(my_pass + i, passes)), device_id_type=MESH
        )

    blank = jnp.zeros((PAD, lanes), F32)
    put(image_b, 0, blank)

    per = 2 * pulses
    lane_block = lane_iota(8, lanes)[:1] >> (per.bit_length() - 1)
    for fetch in fetches[:7]:
        fetch.wait()
    for level in range(local):
        prepare(
            level, 2**level, lane_block * block, block // 8, cells, params, w_ref, table_ref
        )

    fetches[7].wait()
    depth = up(block + taps_count - 1, LANES)
    taps = chirp[...].astype(F32)
    sub = row_iota(8, depth)
    for part in range(2):
        wide_row = jnp.concatenate(
            [
                jnp.broadcast_to(taps[part : part + 1], (8, taps_count)),
                jnp.zeros((8, depth - taps_count), F32),
            ],
            1,
        )
        base = wide_row
        for s in range(1, 8):
            base = jnp.where(sub == s, pltpu.roll(wide_row, s, 1), base)
        for a in range(0, min(block, LANES), 16):
            pair = [base if a == 0 else pltpu.roll(base, a, 1), pltpu.roll(base, a + 8, 1)]
            rows16 = jnp.concatenate(pair, 0).astype(BF16)
            for b in range(max(block // LANES, 1)):
                if b:
                    rows16 = jnp.concatenate([rows16[:, -LANES:], rows16[:, :-LANES]], 1)
                at = part * block + b * LANES + a
                chirp_rows[at : at + 16, :] = rows16
    fetches[8].wait()
    for pulse in range(pulses):
        echo_rows[2 * pulse : 2 * pulse + 2, :samples] = echo[0, pulse].astype(F32)
    need = block * (n - 1) + depth
    if need > samples:
        echo_rows[:, samples:] = jnp.zeros((per, echo_rows.shape[1] - samples), F32)
    echo_cat = jnp.concatenate(
        [echo_rows[:, k * block : k * block + depth].astype(BF16) for k in range(n)], 0
    )
    p_ref[: 2 * block, :lanes] = lax.dot_general(
        chirp_rows[...], echo_cat, (((1,), (1,)), ((), ())), preferred_element_type=F32
    )
    odd = (lane_iota(8, lanes)[:1] & 1) == 1
    for at in range(0, block, 32):
        crossed = p_ref[block + at : block + at + 32, :lanes]
        put(
            image_a,
            PAD + at,
            p_ref[at : at + 32, :lanes]
            + jnp.where(odd, -pltpu.roll(crossed, 1, 1), pltpu.roll(crossed, lanes - 1, 1)),
        )

    def shifted(ref, begin, rows, q):
        value = take(ref, PAD + begin, rows)
        if q == 0:
            return value
        keep = (lane_block + q >= 0) & (lane_block + q < n)
        return jnp.where(keep, pltpu.roll(value, (-q * per) % lanes, 1), 0.0)

    src, dst = image_a, image_b
    scratch = (z_ref, x_ref, p_ref, w_ref, table_ref)
    for level in range(local):
        put(src, 0, shifted(src, block - PAD, PAD, -1))
        put(src, PAD + block, shifted(src, 0, PAD, 1))
        merge(level, 2**level, 0, block, src, dst, None, params, *scratch)
        src, dst = dst, src
    pieces = []
    at = -halo
    while at < block + halo:
        q = at // block
        end = min(block + halo, (q + 1) * block)
        pieces.append(shifted(src, at - q * block, end - at, q))
        at = end
    send_ap[...] = jnp.concatenate(pieces, 0).T.reshape(n, per, wide)

    pl.semaphore_wait(barrier, n - 1 + passes - 1)
    copies = []
    for i in range(1, n):
        to = lax.rem(me + i, n)
        copy = pltpu.make_async_remote_copy(
            src_ref=send_ap.at[rev(to)],
            dst_ref=recv_ap.at[me],
            send_sem=send_sem.at[i],
            recv_sem=recv_sem.at[i],
            device_id=(to, my_pass),
            device_id_type=MESH,
        )
        copy.start()
        copies.append(copy)
    recv_ap[me] = send_ap[rev(me)]

    origin = rev(me) * block - halo
    margins = [
        halo if digit + 1 == cross else (digit + 1) * reach // 8 * 8 for digit in range(cross)
    ]
    for digit, margin in enumerate(margins):
        level = local + digit
        prepare(
            level,
            2**level,
            origin + margin,
            (wide - 2 * margin) // 8,
            cells,
            params,
            w_ref,
            table_ref,
        )
    fetches[9].wait()
    bases = invert.shape[1]
    real, imag = invert[0], invert[1]
    table = jnp.concatenate(
        [jnp.concatenate([real, imag], 1), jnp.concatenate([-imag, real], 1)], 0
    ).T
    table_high, table_low = split(table)
    row = row_iota(2 * bases, 2 * passes)
    column = lane_iota(2 * bases, 2 * passes)
    chosen = jnp.zeros((2 * bases, 2 * passes), F32)
    for p in range(passes):
        for c in range(2):
            hit = (column == 2 * p + c) & (row == c * bases + baseline[p])
            chosen = jnp.where(hit, 1.0, chosen)
    chosen = chosen.astype(BF16)
    mixer_high = jnp.dot(table_high, chosen, preferred_element_type=F32).astype(BF16)
    mixer_low = jnp.dot(table_low, chosen, preferred_element_type=F32).astype(BF16)
    mixer[...] = jnp.concatenate([mixer_high, mixer_high, mixer_low], 1)
    put(image_a, 0, blank)
    put(image_b, 0, jnp.zeros((PAD + 24, lanes), F32))
    put(image_a, PAD + wide, blank)
    put(image_b, PAD + wide - 24, jnp.zeros((PAD + 24, lanes), F32))

    for copy in copies:
        copy.wait()
    put(image_a, PAD, recv_ap[...].reshape(lanes, wide).T)

    src, dst = image_a, image_b
    valid = (origin, block, halo, cells)
    for digit, margin in enumerate(margins):
        level = local + digit
        merge(level, 2**level, margin, wide - margin, src, dst, valid, params, *scratch)
        src, dst = dst, src

    beams = 2**levels
    share = beams // passes
    spread = LANES // share
    count = block // spread
    rows = [take(src, PAD + halo + s, count, spread) for s in range(spread)]
    group = lane_iota(8, LANES)[:1] >> (share.bit_length() - 1)
    for chunk in range(lanes // LANES):
        held = [value[:, chunk * LANES : (chunk + 1) * LANES] for value in rows]
        step = spread // 2
        while step:
            upper = (group & step) != 0
            moved = list(held)
            for s in range(spread):
                if s & step == 0:
                    low, high = held[s], held[s + step]
                    moved[s] = jnp.where(upper, pltpu.roll(high, step * share, 1), low)
                    moved[s + step] = jnp.where(
                        upper, high, pltpu.roll(low, LANES - step * share, 1)
                    )
            held = moved
            step //= 2
        for k, value in enumerate(held):
            c, b = divmod(chunk * spread + k, passes)
            send_pass[b, c * count : (c + 1) * count] = value
    copies = []
    for i in range(1, passes):
        to = lax.rem(my_pass + i, passes)
        copy = pltpu.make_async_remote_copy(
            src_ref=send_pass.at[to],
            dst_ref=out.at[my_pass],
            send_sem=send_sem2.at[i],
            recv_sem=recv_sem2.at[i],
            device_id=(me, to),
            device_id_type=MESH,
        )
        copy.start()
        copies.append(copy)
    out[my_pass] = send_pass[my_pass]
    for copy in copies:
        copy.wait()


def power_kernel(passes, count, data, mixer, out, power_ref, out_sem):
    heights = out.shape[0]
    weights = mixer[...]
    chunk = min(count, 8)
    copies = []
    view = power_ref.reshape(heights, count, LANES)
    for k, a0 in enumerate(range(0, count, chunk)):
        values = jnp.concatenate(
            [data[pl.ds(a, 2 * passes, stride=count), :] for a in range(a0, a0 + chunk)], 1
        )
        high = values.astype(BF16).astype(F32)
        low = values - high
        stack = jnp.concatenate([high, low, high], 0).astype(BF16)
        tomo = jnp.dot(weights, stack, preferred_element_type=F32)
        power = tomo[:heights] * tomo[:heights] + tomo[heights:] * tomo[heights:]
        for a in range(chunk):
            power_ref[pl.ds(a0 + a, heights, stride=count), :] = power[
                :, a * LANES : (a + 1) * LANES
            ]
        copy = pltpu.make_async_copy(
            view.at[:, pl.ds(a0, chunk), :], out.at[:, pl.ds(a0, chunk), :], out_sem.at[k]
        )
        copy.start()
        copies.append(copy)
    for copy in copies:
        copy.wait()


def body(
    mesh_shape,
    echo,
    chirp,
    pair_swap,
    range_shift,
    angle_shift,
    range_taps,
    angle_taps,
    phase_rates,
    invert,
    baseline_index,
):
    n, passes = mesh_shape["ap"], mesh_shape["pass"]
    pulses, samples = echo.shape[1], echo.shape[3]
    levels = range_taps.shape[0]
    taps_count = chirp.shape[1]
    cells = samples - taps_count
    block = cells // n
    beams = 2**levels
    share = beams // passes
    heights = invert.shape[1]
    count = block * share // LANES
    lanes = n * 2 * pulses
    reach = RMAX + range_taps.shape[2] // 2
    local = pulses.bit_length() - 1
    wide = up(block + 2 * reach * (levels - local), LANES)
    depth = up(block + taps_count - 1, LANES)
    vmem = pl.BlockSpec(memory_space=pltpu.VMEM)
    hbm = pl.BlockSpec(memory_space=pltpu.HBM)
    operands = (
        echo,
        chirp,
        pair_swap,
        jnp.transpose(range_shift, (0, 2, 1)),
        jnp.transpose(angle_shift, (0, 2, 3, 1)),
        range_taps,
        angle_taps,
        jnp.transpose(phase_rates, (1, 2, 3, 0)),
        jnp.transpose(invert, (0, 2, 1)),
        baseline_index,
    )
    held = [
        (pltpu.VMEM if i in (0, 1, 8) else pltpu.SMEM)(operand.shape, operand.dtype)
        for i, operand in enumerate(operands)
    ]
    stacks, mixer = pl.pallas_call(
        functools.partial(image_kernel, (n, passes, pulses, cells, levels)),
        out_shape=(
            jax.ShapeDtypeStruct((passes, 2 * count, LANES), F32),
            jax.ShapeDtypeStruct((2 * heights, 6 * passes), BF16),
        ),
        in_specs=[hbm] * len(operands),
        out_specs=(vmem, vmem),
        scratch_shapes=held
        + [
            pltpu.VMEM((2 * pulses, up(max(samples, block * (n - 1) + depth), LANES)), F32),
            pltpu.VMEM((2 * block, depth), BF16),
            pltpu.VMEM((lanes // LANES, wide + 2 * PAD, LANES), F32),
            pltpu.VMEM((lanes // LANES, wide + 2 * PAD, LANES), F32),
            pltpu.VMEM((lanes // LANES, wide + 8, LANES), F32),
            pltpu.VMEM((wide, 3 * lanes), BF16),
            pltpu.VMEM((max(wide, 2 * block), 4 * lanes), F32),
            pltpu.VMEM((levels, 3 * lanes, 4 * lanes), BF16),
            pltpu.VMEM((levels, 2, 2, 8 + up(wide // 8, 8), lanes), F32),
            pltpu.VMEM((n, 2 * pulses, wide), F32),
            pltpu.VMEM((n, 2 * pulses, wide), F32),
            pltpu.VMEM((passes, 2 * count, LANES), F32),
            pltpu.SemaphoreType.DMA((len(operands),)),
            pltpu.SemaphoreType.DMA((n,)),
            pltpu.SemaphoreType.DMA((n,)),
            pltpu.SemaphoreType.DMA((passes,)),
            pltpu.SemaphoreType.DMA((passes,)),
        ],
        compiler_params=pltpu.CompilerParams(
            collective_id=0,
            has_side_effects=True,
            vmem_limit_bytes=min(56 * 2**20, 16 * 2**20 + 24 * levels * lanes * lanes),
        ),
        name="image",
    )(*operands)
    power = pl.pallas_call(
        functools.partial(power_kernel, passes, count),
        out_shape=jax.ShapeDtypeStruct((heights, count, LANES), F32),
        in_specs=[vmem, vmem],
        out_specs=hbm,
        scratch_shapes=[
            pltpu.VMEM((heights * count, LANES), F32),
            pltpu.SemaphoreType.DMA((count,)),
        ],
        compiler_params=pltpu.CompilerParams(vmem_limit_bytes=32 * 2**20),
        name="power",
    )(stacks.reshape(passes * 2 * count, LANES), mixer)
    return power.reshape(1, heights, 1, block * share)


def solution(mesh):
    return jax.shard_map(
        functools.partial(body, dict(mesh.shape)),
        mesh=mesh,
        in_specs=(
            P("pass", "ap", None, None),
            P(),
            P("pass", None),
            P("pass", None, None),
            P("pass", None, None, None),
            P(),
            P(),
            P(),
            P(),
            P(),
        ),
        out_specs=P("pass", None, "ap", None),
        check_vma=False,
    )
```

```python
import functools
import math

import jax
import jax.numpy as jnp
from jax import lax
from jax.experimental import pallas as pl
from jax.experimental.pallas import tpu as pltpu
from jax.sharding import PartitionSpec as P

RMAX = 16
PAD = 24
F32 = jnp.float32
BF16 = jnp.bfloat16
MESH = pl.DeviceIdType.MESH
LANES = 128


def up(value, unit):
    return -(-value // unit) * unit


def lane_iota(rows, lanes):
    return lax.broadcasted_iota(jnp.int32, (rows, lanes), 1)


def row_iota(rows, lanes):
    return lax.broadcasted_iota(jnp.int32, (rows, lanes), 0)


def sincos(theta):
    turns = jnp.floor(theta * (2.0 / math.pi) + 0.5)
    rest = theta - turns * 1.5703125
    rest = rest - turns * 4.837512969970703125e-4
    rest = rest - turns * 7.549789948768648e-8
    sq = rest * rest
    sine = rest + rest * sq * (
        -1.6666654611e-1 + sq * (8.3321608736e-3 + sq * -1.9515295891e-4)
    )
    cosine = 1.0 - 0.5 * sq + sq * sq * (
        4.166664568298827e-2 + sq * (-1.388731625493765e-3 + sq * 2.443315711809948e-5)
    )
    quadrant = turns.astype(jnp.int32) & 3
    odd = (quadrant & 1) == 1
    sin_out = jnp.where(odd, cosine, sine)
    cos_out = jnp.where(odd, sine, cosine)
    sin_out = jnp.where(quadrant >= 2, -sin_out, sin_out)
    cos_out = jnp.where((quadrant == 1) | (quadrant == 2), -cos_out, cos_out)
    return sin_out, cos_out


def take(ref, begin, rows, stride=None):
    where = pl.ds(begin, rows) if stride is None else pl.ds(begin, rows, stride=stride)
    return jnp.concatenate([ref[k, where, :] for k in range(ref.shape[0])], 1)


def put(ref, begin, value):
    for k in range(ref.shape[0]):
        ref[k, begin : begin + value.shape[0]] = value[:, k * LANES : (k + 1) * LANES]


def split(value):
    high = value.astype(BF16)
    low = (value - high.astype(F32)).astype(BF16)
    return high, low


def roles(swap_ref, level):
    swap = swap_ref[0, level]
    return [swap, 1 - swap]


def prepare(level, beams, origin, tiles, cells, params, w_ref, table_ref):
    swap_ref, _, angle_shift, _, angle_taps, rates = params
    lanes = w_ref.shape[2] // 4
    role = roles(swap_ref, level)
    taps_count = angle_taps.shape[3]
    q = lane_iota(8, lanes)[:1] & (2 * beams - 1)
    h_odd = (q & 1) == 1
    j_out = q >> 1
    log_beams = beams.bit_length() - 1
    part_out = (lane_iota(16, lanes) >> (log_beams + 1)) & 1
    group_out = lane_iota(16, lanes) >> (log_beams + 2)
    core_rows = max(16, beams)
    j_in = row_iota(core_rows, lanes) & (beams - 1)
    cores = []
    for e in role:
        offset = jnp.where(
            h_odd, angle_shift[0, e, 1, level], angle_shift[0, e, 0, level]
        ) - (taps_count // 2 - 1)
        core = jnp.zeros((core_rows, lanes), F32)
        for u in range(taps_count):
            source = jnp.clip(j_out + offset + u, 0, beams - 1)
            weight = jnp.where(
                h_odd, angle_taps[level, e, 1, u], angle_taps[level, e, 0, u]
            ) * math.sqrt(0.5)
            core = core + jnp.where(j_in == source, weight, 0.0)
        cores.append(core)
    for at in range(0, lanes, 16):
        in_row = at + row_iota(16, lanes)
        group_in = in_row >> (log_beams + 1)
        same_part = ((in_row >> log_beams) & 1) == part_out
        for c in range(2):
            core = cores[c][at % core_rows : at % core_rows + 16]
            full = jnp.where(group_in == 2 * group_out + c, core, 0.0)
            plain = jnp.where(same_part, full, 0.0)
            turned = jnp.where(same_part, 0.0, jnp.where(part_out == 0, -full, full))
            for place, value in ((c, plain), (2 + c, turned)):
                high, low = split(value)
                columns = slice(place * lanes, (place + 1) * lanes)
                w_ref[level, at : at + 16, columns] = high
                w_ref[level, lanes + at : lanes + at + 16, columns] = high
                w_ref[level, 2 * lanes + at : 2 * lanes + at + 16, columns] = low

    beam_at = q.astype(F32) * (1.0 / (2 * beams))
    row = row_iota(8, lanes)
    groups = -(-tiles // 8)
    for c, e in enumerate(role):
        slope = jnp.where(h_odd, rates[e, 1, 0, level], rates[e, 0, 0, level]) * (8.0 / cells)
        tilt = jnp.where(h_odd, rates[e, 1, 1, level], rates[e, 0, 1, level]) * 8.0
        first = slope * (origin + row).astype(F32) + tilt * beam_at
        along = slope * (8 * row).astype(F32)
        steps = slope * (64 << row).astype(F32)
        sines, cosines = sincos(jnp.concatenate([first, along, steps], 0))
        table_ref[level, c, 0, :8] = cosines[:8]
        table_ref[level, c, 1, :8] = sines[:8]
        held = [(cosines[8:16], sines[8:16])]
        m = 0
        while len(held) < groups:
            s_step, c_step = sines[16 + m : 17 + m], cosines[16 + m : 17 + m]
            for c_old, s_old in held[: groups - len(held)]:
                held.append((c_old * c_step - s_old * s_step, s_old * c_step + c_old * s_step))
            m += 1
        for k, (cosine, sine) in enumerate(held):
            table_ref[level, c, 0, 8 + 8 * k : 16 + 8 * k] = cosine
            table_ref[level, c, 1, 8 + 8 * k : 16 + 8 * k] = sine


def merge(level, beams, lo, hi, src, dst, valid, params, z_ref, x_ref, p_ref, w_ref, table_ref):
    swap_ref, range_shift, _, range_taps, _, _ = params
    lanes = src.shape[0] * LANES
    rows = hi - lo
    role = roles(swap_ref, level)
    child = (lane_iota(8, lanes)[:1] >> beams.bit_length()) & 1
    first = child == 0
    taps_count = range_taps.shape[2]
    o = taps_count // 2 - 1
    starts = [PAD + lo - o + range_shift[0, e, level] for e in role]
    for at in range(0, rows + 8, 64):
        n = min(64, rows + 8 - at)
        put(z_ref, at, jnp.where(first, take(src, starts[0] + at, n), take(src, starts[1] + at, n)))
    weights = [
        jnp.where(first, range_taps[level, role[0], t], range_taps[level, role[1], t])
        for t in range(taps_count)
    ]
    for at in range(0, rows, 32):
        n = min(32, rows - at)
        ranged = weights[0] * take(z_ref, at, n)
        for t in range(1, taps_count):
            ranged = ranged + weights[t] * take(z_ref, at + t, n)
        high, low = split(ranged)
        x_ref[at : at + n, :lanes] = high
        x_ref[at : at + n, lanes : 2 * lanes] = low
        x_ref[at : at + n, 2 * lanes :] = high
    p_ref[:rows] = jnp.dot(x_ref[:rows], w_ref[level], preferred_element_type=F32)
    base = [(table_ref[level, c, 0, :8], table_ref[level, c, 1, :8]) for c in range(2)]
    for a in range(rows // 8):
        total = None
        for c in range(2):
            c_step = table_ref[level, c, 0, 8 + a : 9 + a]
            s_step = table_ref[level, c, 1, 8 + a : 9 + a]
            c_base, s_base = base[c]
            cosine = c_base * c_step - s_base * s_step
            sine = s_base * c_step + c_base * s_step
            plain = p_ref[8 * a : 8 * a + 8, c * lanes : (c + 1) * lanes]
            turned = p_ref[8 * a : 8 * a + 8, (2 + c) * lanes : (3 + c) * lanes]
            term = cosine * plain + sine * turned
            total = term if c == 0 else total + term
        at = lo + 8 * a
        if valid is not None:
            origin, block, halo, cells = valid
            if at < halo or at >= halo + block:
                cell = origin + at + row_iota(8, lanes)
                total = jnp.where((cell >= 0) & (cell < cells), total, 0.0)
        put(dst, PAD + at, total)


def image_kernel(
    sizes,
    echo_in,
    chirp_in,
    swap_in,
    range_shift_in,
    angle_shift_in,
    range_taps_in,
    angle_taps_in,
    rates_in,
    invert_in,
    baseline_in,
    out,
    mixer,
    echo,
    chirp,
    swap_ref,
    range_shift,
    angle_shift,
    range_taps,
    angle_taps,
    rates,
    invert,
    baseline,
    echo_rows,
    chirp_rows,
    image_a,
    image_b,
    z_ref,
    x_ref,
    p_ref,
    w_ref,
    table_ref,
    send_ap,
    recv_ap,
    send_pass,
    in_sem,
    send_sem,
    recv_sem,
    send_sem2,
    recv_sem2,
):
    n, passes, pulses, cells, levels = sizes
    lanes = n * 2 * pulses
    taps_count = chirp.shape[1]
    samples = echo.shape[3]
    block = cells // n
    reach = RMAX + range_taps.shape[2] // 2
    local = pulses.bit_length() - 1
    cross = levels - local
    wide = up(block + 2 * reach * cross, LANES)
    halo = (wide - block) // 2
    me = lax.axis_index("ap")
    my_pass = lax.axis_index("pass")
    params = (swap_ref, range_shift, angle_shift, range_taps, angle_taps, rates)

    def rev(index):
        total = 0
        for digit in range(cross):
            total = total + (index // 2**digit) % 2 * 2 ** (cross - 1 - digit)
        return total

    pairs = [
        (swap_in, swap_ref),
        (angle_shift_in, angle_shift),
        (angle_taps_in, angle_taps),
        (rates_in, rates),
        (range_shift_in, range_shift),
        (range_taps_in, range_taps),
        (baseline_in, baseline),
        (chirp_in, chirp),
        (echo_in, echo),
        (invert_in, invert),
    ]
    fetches = [
        pltpu.make_async_copy(there, here, in_sem.at[i]) for i, (there, here) in enumerate(pairs)
    ]
    for fetch in fetches:
        fetch.start()

    barrier = pltpu.get_barrier_semaphore()
    for i in range(1, n):
        pl.semaphore_signal(
            barrier, inc=1, device_id=(lax.rem(me + i, n), my_pass), device_id_type=MESH
        )
    for i in range(1, passes):
        pl.semaphore_signal(
            barrier, inc=1, device_id=(me, lax.rem(my_pass + i, passes)), device_id_type=MESH
        )

    blank = jnp.zeros((PAD, lanes), F32)
    put(image_b, 0, blank)

    per = 2 * pulses
    lane_block = lane_iota(8, lanes)[:1] >> (per.bit_length() - 1)
    for fetch in fetches[:7]:
        fetch.wait()
    for level in range(local):
        prepare(
            level, 2**level, lane_block * block, block // 8, cells, params, w_ref, table_ref
        )

    fetches[7].wait()
    depth = up(block + taps_count - 1, LANES)
    taps = chirp[...].astype(F32)
    sub = row_iota(8, depth)
    for part in range(2):
        wide_row = jnp.concatenate(
            [
                jnp.broadcast_to(taps[part : part + 1], (8, taps_count)),
                jnp.zeros((8, depth - taps_count), F32),
            ],
            1,
        )
        base = wide_row
        for s in range(1, 8):
            base = jnp.where(sub == s, pltpu.roll(wide_row, s, 1), base)
        for a in range(0, min(block, LANES), 16):
            pair = [base if a == 0 else pltpu.roll(base, a, 1), pltpu.roll(base, a + 8, 1)]
            rows16 = jnp.concatenate(pair, 0).astype(BF16)
            for b in range(max(block // LANES, 1)):
                if b:
                    rows16 = jnp.concatenate([rows16[:, -LANES:], rows16[:, :-LANES]], 1)
                at = part * block + b * LANES + a
                chirp_rows[at : at + 16, :] = rows16
    fetches[8].wait()
    for pulse in range(pulses):
        echo_rows[2 * pulse : 2 * pulse + 2, :samples] = echo[0, pulse].astype(F32)
    need = block * (n - 1) + depth
    if need > samples:
        echo_rows[:, samples:] = jnp.zeros((per, echo_rows.shape[1] - samples), F32)
    echo_cat = jnp.concatenate(
        [echo_rows[:, k * block : k * block + depth].astype(BF16) for k in range(n)], 0
    )
    p_ref[: 2 * block, :lanes] = lax.dot_general(
        chirp_rows[...], echo_cat, (((1,), (1,)), ((), ())), preferred_element_type=F32
    )
    odd = (lane_iota(8, lanes)[:1] & 1) == 1
    for at in range(0, block, 32):
        crossed = p_ref[block + at : block + at + 32, :lanes]
        put(
            image_a,
            PAD + at,
            p_ref[at : at + 32, :lanes]
            + jnp.where(odd, -pltpu.roll(crossed, 1, 1), pltpu.roll(crossed, lanes - 1, 1)),
        )

    def shifted(ref, begin, rows, q):
        value = take(ref, PAD + begin, rows)
        if q == 0:
            return value
        keep = (lane_block + q >= 0) & (lane_block + q < n)
        return jnp.where(keep, pltpu.roll(value, (-q * per) % lanes, 1), 0.0)

    src, dst = image_a, image_b
    scratch = (z_ref, x_ref, p_ref, w_ref, table_ref)
    for level in range(local):
        put(src, 0, shifted(src, block - PAD, PAD, -1))
        put(src, PAD + block, shifted(src, 0, PAD, 1))
        merge(level, 2**level, 0, block, src, dst, None, params, *scratch)
        src, dst = dst, src
    pieces = []
    at = -halo
    while at < block + halo:
        q = at // block
        end = min(block + halo, (q + 1) * block)
        pieces.append(shifted(src, at - q * block, end - at, q))
        at = end
    send_ap[...] = jnp.concatenate(pieces, 0).T.reshape(n, per, wide)

    pl.semaphore_wait(barrier, n - 1 + passes - 1)
    copies = []
    for i in range(1, n):
        to = lax.rem(me + i, n)
        copy = pltpu.make_async_remote_copy(
            src_ref=send_ap.at[rev(to)],
            dst_ref=recv_ap.at[me],
            send_sem=send_sem.at[i],
            recv_sem=recv_sem.at[i],
            device_id=(to, my_pass),
            device_id_type=MESH,
        )
        copy.start()
        copies.append(copy)
    recv_ap[me] = send_ap[rev(me)]

    origin = rev(me) * block - halo
    margins = [
        halo if digit + 1 == cross else (digit + 1) * reach // 8 * 8 for digit in range(cross)
    ]
    for digit, margin in enumerate(margins):
        level = local + digit
        prepare(
            level,
            2**level,
            origin + margin,
            (wide - 2 * margin) // 8,
            cells,
            params,
            w_ref,
            table_ref,
        )
    fetches[9].wait()
    bases = invert.shape[1]
    real, imag = invert[0], invert[1]
    table = jnp.concatenate(
        [jnp.concatenate([real, imag], 1), jnp.concatenate([-imag, real], 1)], 0
    ).T
    table_high, table_low = split(table)
    row = row_iota(2 * bases, 2 * passes)
    column = lane_iota(2 * bases, 2 * passes)
    chosen = jnp.zeros((2 * bases, 2 * passes), F32)
    for p in range(passes):
        for c in range(2):
            hit = (column == 2 * p + c) & (row == c * bases + baseline[p])
            chosen = jnp.where(hit, 1.0, chosen)
    chosen = chosen.astype(BF16)
    mixer_high = jnp.dot(table_high, chosen, preferred_element_type=F32).astype(BF16)
    mixer_low = jnp.dot(table_low, chosen, preferred_element_type=F32).astype(BF16)
    mixer[...] = jnp.concatenate([mixer_high, mixer_high, mixer_low], 1)
    put(image_a, 0, blank)
    put(image_b, 0, jnp.zeros((PAD + 24, lanes), F32))
    put(image_a, PAD + wide, blank)
    put(image_b, PAD + wide - 24, jnp.zeros((PAD + 24, lanes), F32))

    for copy in copies:
        copy.wait()
    put(image_a, PAD, recv_ap[...].reshape(lanes, wide).T)

    src, dst = image_a, image_b
    valid = (origin, block, halo, cells)
    for digit, margin in enumerate(margins):
        level = local + digit
        merge(level, 2**level, margin, wide - margin, src, dst, valid, params, *scratch)
        src, dst = dst, src

    beams = 2**levels
    share = beams // passes
    spread = LANES // share
    count = block // spread
    rows = [take(src, PAD + halo + s, count, spread) for s in range(spread)]
    group = lane_iota(8, LANES)[:1] >> (share.bit_length() - 1)
    for chunk in range(lanes // LANES):
        held = [value[:, chunk * LANES : (chunk + 1) * LANES] for value in rows]
        step = spread // 2
        while step:
            upper = (group & step) != 0
            moved = list(held)
            for s in range(spread):
                if s & step == 0:
                    low, high = held[s], held[s + step]
                    moved[s] = jnp.where(upper, pltpu.roll(high, step * share, 1), low)
                    moved[s + step] = jnp.where(
                        upper, high, pltpu.roll(low, LANES - step * share, 1)
                    )
            held = moved
            step //= 2
        for k, value in enumerate(held):
            c, b = divmod(chunk * spread + k, passes)
            send_pass[b, c * count : (c + 1) * count] = value
    copies = []
    for i in range(1, passes):
        to = lax.rem(my_pass + i, passes)
        copy = pltpu.make_async_remote_copy(
            src_ref=send_pass.at[to],
            dst_ref=out.at[my_pass],
            send_sem=send_sem2.at[i],
            recv_sem=recv_sem2.at[i],
            device_id=(me, to),
            device_id_type=MESH,
        )
        copy.start()
        copies.append(copy)
    out[my_pass] = send_pass[my_pass]
    for copy in copies:
        copy.wait()


def power_kernel(passes, count, data, mixer, out, power_ref, out_sem):
    heights = out.shape[0]
    weights = mixer[...]
    chunk = min(count, 8)
    copies = []
    view = power_ref.reshape(heights, count, LANES)
    for k, a0 in enumerate(range(0, count, chunk)):
        values = jnp.concatenate(
            [data[pl.ds(a, 2 * passes, stride=count), :] for a in range(a0, a0 + chunk)], 1
        )
        high = values.astype(BF16).astype(F32)
        low = values - high
        stack = jnp.concatenate([high, low, high], 0).astype(BF16)
        tomo = jnp.dot(weights, stack, preferred_element_type=F32)
        power = tomo[:heights] * tomo[:heights] + tomo[heights:] * tomo[heights:]
        for a in range(chunk):
            power_ref[pl.ds(a0 + a, heights, stride=count), :] = power[
                :, a * LANES : (a + 1) * LANES
            ]
        copy = pltpu.make_async_copy(
            view.at[:, pl.ds(a0, chunk), :], out.at[:, pl.ds(a0, chunk), :], out_sem.at[k]
        )
        copy.start()
        copies.append(copy)
    for copy in copies:
        copy.wait()


def body(
    mesh_shape,
    echo,
    chirp,
    pair_swap,
    range_shift,
    angle_shift,
    range_taps,
    angle_taps,
    phase_rates,
    invert,
    baseline_index,
):
    n, passes = mesh_shape["ap"], mesh_shape["pass"]
    pulses, samples = echo.shape[1], echo.shape[3]
    levels = range_taps.shape[0]
    taps_count = chirp.shape[1]
    cells = samples - taps_count
    block = cells // n
    beams = 2**levels
    share = beams // passes
    heights = invert.shape[1]
    count = block * share // LANES
    lanes = n * 2 * pulses
    reach = RMAX + range_taps.shape[2] // 2
    local = pulses.bit_length() - 1
    wide = up(block + 2 * reach * (levels - local), LANES)
    depth = up(block + taps_count - 1, LANES)
    vmem = pl.BlockSpec(memory_space=pltpu.VMEM)
    hbm = pl.BlockSpec(memory_space=pltpu.HBM)
    operands = (
        echo,
        chirp,
        pair_swap,
        jnp.transpose(range_shift, (0, 2, 1)),
        jnp.transpose(angle_shift, (0, 2, 3, 1)),
        range_taps,
        angle_taps,
        jnp.transpose(phase_rates, (1, 2, 3, 0)),
        jnp.transpose(invert, (0, 2, 1)),
        baseline_index,
    )
    held = [
        (pltpu.VMEM if i in (0, 1, 8) else pltpu.SMEM)(operand.shape, operand.dtype)
        for i, operand in enumerate(operands)
    ]
    stacks, mixer = pl.pallas_call(
        functools.partial(image_kernel, (n, passes, pulses, cells, levels)),
        out_shape=(
            jax.ShapeDtypeStruct((passes, 2 * count, LANES), F32),
            jax.ShapeDtypeStruct((2 * heights, 6 * passes), BF16),
        ),
        in_specs=[hbm] * len(operands),
        out_specs=(vmem, vmem),
        scratch_shapes=held
        + [
            pltpu.VMEM((2 * pulses, up(max(samples, block * (n - 1) + depth), LANES)), F32),
            pltpu.VMEM((2 * block, depth), BF16),
            pltpu.VMEM((lanes // LANES, wide + 2 * PAD, LANES), F32),
            pltpu.VMEM((lanes // LANES, wide + 2 * PAD, LANES), F32),
            pltpu.VMEM((lanes // LANES, wide + 8, LANES), F32),
            pltpu.VMEM((wide, 3 * lanes), BF16),
            pltpu.VMEM((max(wide, 2 * block), 4 * lanes), F32),
            pltpu.VMEM((levels, 3 * lanes, 4 * lanes), BF16),
            pltpu.VMEM((levels, 2, 2, 8 + up(wide // 8, 8), lanes), F32),
            pltpu.VMEM((n, 2 * pulses, wide), F32),
            pltpu.VMEM((n, 2 * pulses, wide), F32),
            pltpu.VMEM((passes, 2 * count, LANES), F32),
            pltpu.SemaphoreType.DMA((len(operands),)),
            pltpu.SemaphoreType.DMA((n,)),
            pltpu.SemaphoreType.DMA((n,)),
            pltpu.SemaphoreType.DMA((passes,)),
            pltpu.SemaphoreType.DMA((passes,)),
        ],
        compiler_params=pltpu.CompilerParams(
            collective_id=0,
            has_side_effects=True,
            vmem_limit_bytes=min(56 * 2**20, 16 * 2**20 + 24 * levels * lanes * lanes),
        ),
        name="image",
    )(*[pltpu.with_memory_space_constraint(operand, pltpu.HBM) for operand in operands])
    power = pl.pallas_call(
        functools.partial(power_kernel, passes, count),
        out_shape=jax.ShapeDtypeStruct((heights, count, LANES), F32),
        in_specs=[vmem, vmem],
        out_specs=hbm,
        scratch_shapes=[
            pltpu.VMEM((heights * count, LANES), F32),
            pltpu.SemaphoreType.DMA((count,)),
        ],
        compiler_params=pltpu.CompilerParams(vmem_limit_bytes=32 * 2**20),
        name="power",
    )(stacks.reshape(passes * 2 * count, LANES), mixer)
    return power.reshape(1, heights, 1, block * share)


def solution(mesh):
    return jax.shard_map(
        functools.partial(body, dict(mesh.shape)),
        mesh=mesh,
        in_specs=(
            P("pass", "ap", None, None),
            P(),
            P("pass", None),
            P("pass", None, None),
            P("pass", None, None, None),
            P(),
            P(),
            P(),
            P(),
            P(),
        ),
        out_specs=P("pass", None, "ap", None),
        check_vma=False,
    )
```

```python
import functools
import math

import jax
import jax.numpy as jnp
from jax import lax
from jax.experimental import pallas as pl
from jax.experimental.pallas import tpu as pltpu
from jax.sharding import PartitionSpec as P

RMAX = 16
PAD = 24
F32 = jnp.float32
BF16 = jnp.bfloat16
MESH = pl.DeviceIdType.MESH
LANES = 128


def up(value, unit):
    return -(-value // unit) * unit


def lane_iota(rows, lanes):
    return lax.broadcasted_iota(jnp.int32, (rows, lanes), 1)


def row_iota(rows, lanes):
    return lax.broadcasted_iota(jnp.int32, (rows, lanes), 0)


def sincos(theta):
    turns = jnp.floor(theta * (2.0 / math.pi) + 0.5)
    rest = theta - turns * 1.5703125
    rest = rest - turns * 4.837512969970703125e-4
    rest = rest - turns * 7.549789948768648e-8
    sq = rest * rest
    sine = rest + rest * sq * (
        -1.6666654611e-1 + sq * (8.3321608736e-3 + sq * -1.9515295891e-4)
    )
    cosine = 1.0 - 0.5 * sq + sq * sq * (
        4.166664568298827e-2 + sq * (-1.388731625493765e-3 + sq * 2.443315711809948e-5)
    )
    quadrant = turns.astype(jnp.int32) & 3
    odd = (quadrant & 1) == 1
    sin_out = jnp.where(odd, cosine, sine)
    cos_out = jnp.where(odd, sine, cosine)
    sin_out = jnp.where(quadrant >= 2, -sin_out, sin_out)
    cos_out = jnp.where((quadrant == 1) | (quadrant == 2), -cos_out, cos_out)
    return sin_out, cos_out


def take(ref, begin, rows, stride=None):
    where = pl.ds(begin, rows) if stride is None else pl.ds(begin, rows, stride=stride)
    return jnp.concatenate([ref[k, where, :] for k in range(ref.shape[0])], 1)


def put(ref, begin, value):
    for k in range(ref.shape[0]):
        ref[k, begin : begin + value.shape[0]] = value[:, k * LANES : (k + 1) * LANES]


def split(value):
    high = value.astype(BF16)
    low = (value - high.astype(F32)).astype(BF16)
    return high, low


def roles(swap_ref, level):
    swap = swap_ref[0, level]
    return [swap, 1 - swap]


def prepare(level, beams, origin, tiles, cells, params, w_ref, table_ref):
    swap_ref, _, angle_shift, _, angle_taps, rates = params
    lanes = w_ref.shape[2] // 4
    role = roles(swap_ref, level)
    taps_count = angle_taps.shape[3]
    q = lane_iota(8, lanes)[:1] & (2 * beams - 1)
    h_odd = (q & 1) == 1
    j_out = q >> 1
    log_beams = beams.bit_length() - 1
    part_out = (lane_iota(16, lanes) >> (log_beams + 1)) & 1
    group_out = lane_iota(16, lanes) >> (log_beams + 2)
    core_rows = max(16, beams)
    j_in = row_iota(core_rows, lanes) & (beams - 1)
    cores = []
    for e in role:
        offset = jnp.where(
            h_odd, angle_shift[0, e, 1, level], angle_shift[0, e, 0, level]
        ) - (taps_count // 2 - 1)
        core = jnp.zeros((core_rows, lanes), F32)
        for u in range(taps_count):
            source = jnp.clip(j_out + offset + u, 0, beams - 1)
            weight = jnp.where(
                h_odd, angle_taps[level, e, 1, u], angle_taps[level, e, 0, u]
            ) * math.sqrt(0.5)
            core = core + jnp.where(j_in == source, weight, 0.0)
        cores.append(core)
    for at in range(0, lanes, 16):
        in_row = at + row_iota(16, lanes)
        group_in = in_row >> (log_beams + 1)
        same_part = ((in_row >> log_beams) & 1) == part_out
        for c in range(2):
            core = cores[c][at % core_rows : at % core_rows + 16]
            full = jnp.where(group_in == 2 * group_out + c, core, 0.0)
            plain = jnp.where(same_part, full, 0.0)
            turned = jnp.where(same_part, 0.0, jnp.where(part_out == 0, -full, full))
            for place, value in ((c, plain), (2 + c, turned)):
                high, low = split(value)
                columns = slice(place * lanes, (place + 1) * lanes)
                w_ref[level, at : at + 16, columns] = high
                w_ref[level, lanes + at : lanes + at + 16, columns] = high
                w_ref[level, 2 * lanes + at : 2 * lanes + at + 16, columns] = low

    beam_at = q.astype(F32) * (1.0 / (2 * beams))
    row = row_iota(8, lanes)
    groups = -(-tiles // 8)
    for c, e in enumerate(role):
        slope = jnp.where(h_odd, rates[e, 1, 0, level], rates[e, 0, 0, level]) * (8.0 / cells)
        tilt = jnp.where(h_odd, rates[e, 1, 1, level], rates[e, 0, 1, level]) * 8.0
        first = slope * (origin + row).astype(F32) + tilt * beam_at
        along = slope * (8 * row).astype(F32)
        steps = slope * (64 << row).astype(F32)
        sines, cosines = sincos(jnp.concatenate([first, along, steps], 0))
        table_ref[level, c, 0, :8] = cosines[:8]
        table_ref[level, c, 1, :8] = sines[:8]
        held = [(cosines[8:16], sines[8:16])]
        m = 0
        while len(held) < groups:
            s_step, c_step = sines[16 + m : 17 + m], cosines[16 + m : 17 + m]
            for c_old, s_old in held[: groups - len(held)]:
                held.append((c_old * c_step - s_old * s_step, s_old * c_step + c_old * s_step))
            m += 1
        for k, (cosine, sine) in enumerate(held):
            table_ref[level, c, 0, 8 + 8 * k : 16 + 8 * k] = cosine
            table_ref[level, c, 1, 8 + 8 * k : 16 + 8 * k] = sine


def merge(
    level, beams, lo, hi, src, dst, valid, params, z_ref, x_ref, p_ref, w_ref, table_ref, skip=0
):
    swap_ref, range_shift, _, range_taps, _, _ = params
    lanes = src.shape[0] * LANES
    rows = hi - lo
    role = roles(swap_ref, level)
    child = (lane_iota(8, lanes)[:1] >> beams.bit_length()) & 1
    first = child == 0
    taps_count = range_taps.shape[2]
    o = taps_count // 2 - 1
    starts = [PAD + lo - o + range_shift[0, e, level] for e in role]
    for at in range(0, rows + 8, 64):
        n = min(64, rows + 8 - at)
        put(z_ref, at, jnp.where(first, take(src, starts[0] + at, n), take(src, starts[1] + at, n)))
    weights = [
        jnp.where(first, range_taps[level, role[0], t], range_taps[level, role[1], t])
        for t in range(taps_count)
    ]
    for at in range(0, rows, 32):
        n = min(32, rows - at)
        ranged = weights[0] * take(z_ref, at, n)
        for t in range(1, taps_count):
            ranged = ranged + weights[t] * take(z_ref, at + t, n)
        high, low = split(ranged)
        x_ref[at : at + n, :lanes] = high
        x_ref[at : at + n, lanes : 2 * lanes] = low
        x_ref[at : at + n, 2 * lanes :] = high
    p_ref[:rows] = jnp.dot(x_ref[:rows], w_ref[level], preferred_element_type=F32)
    base = [(table_ref[level, c, 0, :8], table_ref[level, c, 1, :8]) for c in range(2)]
    for a in range(rows // 8):
        total = None
        for c in range(2):
            c_step = table_ref[level, c, 0, 8 + skip + a : 9 + skip + a]
            s_step = table_ref[level, c, 1, 8 + skip + a : 9 + skip + a]
            c_base, s_base = base[c]
            cosine = c_base * c_step - s_base * s_step
            sine = s_base * c_step + c_base * s_step
            plain = p_ref[8 * a : 8 * a + 8, c * lanes : (c + 1) * lanes]
            turned = p_ref[8 * a : 8 * a + 8, (2 + c) * lanes : (3 + c) * lanes]
            term = cosine * plain + sine * turned
            total = term if c == 0 else total + term
        at = lo + 8 * a
        if valid is not None:
            origin, block, halo, cells = valid
            if at < halo or at >= halo + block:
                cell = origin + at + row_iota(8, lanes)
                total = jnp.where((cell >= 0) & (cell < cells), total, 0.0)
        put(dst, PAD + at, total)


def image_kernel(
    sizes,
    echo_in,
    chirp_in,
    swap_in,
    range_shift_in,
    angle_shift_in,
    range_taps_in,
    angle_taps_in,
    rates_in,
    invert_in,
    baseline_in,
    out,
    mixer,
    echo,
    chirp,
    swap_ref,
    range_shift,
    angle_shift,
    range_taps,
    angle_taps,
    rates,
    invert,
    baseline,
    echo_rows,
    chirp_rows,
    image_a,
    image_b,
    z_ref,
    x_ref,
    p_ref,
    w_ref,
    table_ref,
    send_ap,
    recv_ap,
    send_pass,
    in_sem,
    send_sem,
    recv_sem,
    send_sem2,
    recv_sem2,
):
    n, passes, pulses, cells, levels = sizes
    lanes = n * 2 * pulses
    taps_count = chirp.shape[1]
    samples = echo.shape[3]
    block = cells // n
    reach = RMAX + range_taps.shape[2] // 2
    local = pulses.bit_length() - 1
    cross = levels - local
    wide = up(block + 2 * reach * cross, LANES)
    halo = (wide - block) // 2
    me = lax.axis_index("ap")
    my_pass = lax.axis_index("pass")
    params = (swap_ref, range_shift, angle_shift, range_taps, angle_taps, rates)

    def rev(index):
        total = 0
        for digit in range(cross):
            total = total + (index // 2**digit) % 2 * 2 ** (cross - 1 - digit)
        return total

    pairs = [
        (swap_in, swap_ref),
        (angle_shift_in, angle_shift),
        (angle_taps_in, angle_taps),
        (rates_in, rates),
        (range_shift_in, range_shift),
        (range_taps_in, range_taps),
        (baseline_in, baseline),
        (chirp_in, chirp),
        (echo_in, echo),
        (invert_in, invert),
    ]
    fetches = [
        pltpu.make_async_copy(there, here, in_sem.at[i]) for i, (there, here) in enumerate(pairs)
    ]
    for fetch in fetches:
        fetch.start()

    barrier = pltpu.get_barrier_semaphore()
    for i in range(1, n):
        pl.semaphore_signal(
            barrier, inc=1, device_id=(lax.rem(me + i, n), my_pass), device_id_type=MESH
        )
    for i in range(1, passes):
        pl.semaphore_signal(
            barrier, inc=1, device_id=(me, lax.rem(my_pass + i, passes)), device_id_type=MESH
        )

    blank = jnp.zeros((PAD, lanes), F32)
    put(image_b, 0, blank)

    per = 2 * pulses
    lane_block = lane_iota(8, lanes)[:1] >> (per.bit_length() - 1)
    for fetch in fetches[:7]:
        fetch.wait()
    for level in range(local):
        prepare(
            level, 2**level, lane_block * block, block // 8, cells, params, w_ref, table_ref
        )

    fetches[7].wait()
    depth = up(block + taps_count - 1, LANES)
    taps = chirp[...].astype(F32)
    sub = row_iota(8, depth)
    for part in range(2):
        wide_row = jnp.concatenate(
            [
                jnp.broadcast_to(taps[part : part + 1], (8, taps_count)),
                jnp.zeros((8, depth - taps_count), F32),
            ],
            1,
        )
        base = wide_row
        for s in range(1, 8):
            base = jnp.where(sub == s, pltpu.roll(wide_row, s, 1), base)
        for a in range(0, min(block, LANES), 16):
            pair = [base if a == 0 else pltpu.roll(base, a, 1), pltpu.roll(base, a + 8, 1)]
            rows16 = jnp.concatenate(pair, 0).astype(BF16)
            for b in range(max(block // LANES, 1)):
                if b:
                    rows16 = jnp.concatenate([rows16[:, -LANES:], rows16[:, :-LANES]], 1)
                at = part * block + b * LANES + a
                chirp_rows[at : at + 16, :] = rows16
    fetches[8].wait()
    for pulse in range(pulses):
        echo_rows[2 * pulse : 2 * pulse + 2, :samples] = echo[0, pulse].astype(F32)
    need = block * (n - 1) + depth
    if need > samples:
        echo_rows[:, samples:] = jnp.zeros((per, echo_rows.shape[1] - samples), F32)
    echo_cat = jnp.concatenate(
        [echo_rows[:, k * block : k * block + depth].astype(BF16) for k in range(n)], 0
    )
    p_ref[: 2 * block, :lanes] = lax.dot_general(
        chirp_rows[...], echo_cat, (((1,), (1,)), ((), ())), preferred_element_type=F32
    )
    odd = (lane_iota(8, lanes)[:1] & 1) == 1
    for at in range(0, block, 32):
        crossed = p_ref[block + at : block + at + 32, :lanes]
        put(
            image_a,
            PAD + at,
            p_ref[at : at + 32, :lanes]
            + jnp.where(odd, -pltpu.roll(crossed, 1, 1), pltpu.roll(crossed, lanes - 1, 1)),
        )

    def shifted(ref, begin, rows, q):
        value = take(ref, PAD + begin, rows)
        if q == 0:
            return value
        keep = (lane_block + q >= 0) & (lane_block + q < n)
        return jnp.where(keep, pltpu.roll(value, (-q * per) % lanes, 1), 0.0)

    src, dst = image_a, image_b
    scratch = (z_ref, x_ref, p_ref, w_ref, table_ref)
    for level in range(local):
        put(src, 0, shifted(src, block - PAD, PAD, -1))
        put(src, PAD + block, shifted(src, 0, PAD, 1))
        merge(level, 2**level, 0, block, src, dst, None, params, *scratch)
        src, dst = dst, src
    pieces = []
    at = -halo
    while at < block + halo:
        q = at // block
        end = min(block + halo, (q + 1) * block)
        pieces.append(shifted(src, at - q * block, end - at, q))
        at = end
    send_ap[...] = jnp.concatenate(pieces, 0).T.reshape(n, per, wide)

    pl.semaphore_wait(barrier, n - 1 + passes - 1)
    copies = []
    for i in range(1, n):
        to = lax.rem(me + i, n)
        copy = pltpu.make_async_remote_copy(
            src_ref=send_ap.at[rev(to)],
            dst_ref=recv_ap.at[me],
            send_sem=send_sem.at[i],
            recv_sem=recv_sem.at[i],
            device_id=(to, my_pass),
            device_id_type=MESH,
        )
        copy.start()
        copies.append(copy)
    recv_ap[me] = send_ap[rev(me)]

    origin = rev(me) * block - halo
    margins = [
        halo if digit + 1 == cross else (digit + 1) * reach // 8 * 8 for digit in range(cross)
    ]
    for digit, margin in enumerate(margins):
        level = local + digit
        prepare(
            level,
            2**level,
            origin + margin,
            (wide - 2 * margin) // 8,
            cells,
            params,
            w_ref,
            table_ref,
        )
    fetches[9].wait()
    bases = invert.shape[1]
    real, imag = invert[0], invert[1]
    table = jnp.concatenate(
        [jnp.concatenate([real, imag], 1), jnp.concatenate([-imag, real], 1)], 0
    ).T
    table_high, table_low = split(table)
    row = row_iota(2 * bases, 2 * passes)
    column = lane_iota(2 * bases, 2 * passes)
    chosen = jnp.zeros((2 * bases, 2 * passes), F32)
    for p in range(passes):
        for c in range(2):
            hit = (column == 2 * p + c) & (row == c * bases + baseline[p])
            chosen = jnp.where(hit, 1.0, chosen)
    chosen = chosen.astype(BF16)
    mixer_high = jnp.dot(table_high, chosen, preferred_element_type=F32).astype(BF16)
    mixer_low = jnp.dot(table_low, chosen, preferred_element_type=F32).astype(BF16)
    mixer[...] = jnp.concatenate([mixer_high, mixer_high, mixer_low], 1)
    put(image_a, 0, blank)
    put(image_b, 0, jnp.zeros((PAD + 24, lanes), F32))
    put(image_a, PAD + wide, blank)
    put(image_b, PAD + wide - 24, jnp.zeros((PAD + 24, lanes), F32))

    for copy in copies:
        copy.wait()
    put(image_a, PAD, recv_ap[...].reshape(lanes, wide).T)

    src, dst = image_a, image_b
    valid = (origin, block, halo, cells)
    for digit, margin in enumerate(margins[:-1]):
        level = local + digit
        merge(level, 2**level, margin, wide - margin, src, dst, valid, params, *scratch)
        src, dst = dst, src

    level = levels - 1
    beams = 2**levels
    share = beams // passes
    spread = LANES // share
    parts, count = out.shape[0], out.shape[2] // 2
    group = lane_iota(8, LANES)[:1] >> (share.bit_length() - 1)
    copies = []
    for part in range(parts):
        lo = halo + part * count * spread
        merge(
            level,
            2**level,
            lo,
            lo + count * spread,
            src,
            dst,
            valid,
            params,
            *scratch,
            skip=part * count * spread // 8,
        )
        rows = [take(dst, PAD + lo + s, count, spread) for s in range(spread)]
        for chunk in range(lanes // LANES):
            held = [value[:, chunk * LANES : (chunk + 1) * LANES] for value in rows]
            step = spread // 2
            while step:
                upper = (group & step) != 0
                moved = list(held)
                for s in range(spread):
                    if s & step == 0:
                        low, high = held[s], held[s + step]
                        moved[s] = jnp.where(upper, pltpu.roll(high, step * share, 1), low)
                        moved[s + step] = jnp.where(
                            upper, high, pltpu.roll(low, LANES - step * share, 1)
                        )
                held = moved
                step //= 2
            for k, value in enumerate(held):
                c, b = divmod(chunk * spread + k, passes)
                send_pass[part, b, c * count : (c + 1) * count] = value
        for i in range(1, passes):
            to = lax.rem(my_pass + i, passes)
            copy = pltpu.make_async_remote_copy(
                src_ref=send_pass.at[part, to],
                dst_ref=out.at[part, my_pass],
                send_sem=send_sem2.at[part * passes + i],
                recv_sem=recv_sem2.at[part * passes + i],
                device_id=(me, to),
                device_id_type=MESH,
            )
            copy.start()
            copies.append(copy)
        out[part, my_pass] = send_pass[part, my_pass]
    for copy in copies:
        copy.wait()


def power_kernel(passes, parts, data, mixer, out, power_ref, out_sem):
    heights, count = out.shape[:2]
    within = count // parts
    pitch = power_ref.shape[0] // heights
    weights = mixer[...]
    chunk = min(count, 8)
    copies = []
    view = power_ref.reshape(heights, pitch, LANES)
    for k, a0 in enumerate(range(0, count, chunk)):
        values = jnp.concatenate(
            [
                data[
                    pl.ds(a // within * within * 2 * passes + a % within, 2 * passes, stride=within),
                    :,
                ]
                for a in range(a0, a0 + chunk)
            ],
            1,
        )
        high = values.astype(BF16).astype(F32)
        low = values - high
        stack = jnp.concatenate([high, low, high], 0).astype(BF16)
        tomo = jnp.dot(weights, stack, preferred_element_type=F32)
        power = tomo[:heights] * tomo[:heights] + tomo[heights:] * tomo[heights:]
        for a in range(chunk):
            power_ref[pl.ds(a0 + a, heights, stride=pitch), :] = power[
                :, a * LANES : (a + 1) * LANES
            ]
        copy = pltpu.make_async_copy(
            view.at[:, pl.ds(a0, chunk), :], out.at[:, pl.ds(a0, chunk), :], out_sem.at[k]
        )
        copy.start()
        copies.append(copy)
    for copy in copies:
        copy.wait()


def body(
    mesh_shape,
    echo,
    chirp,
    pair_swap,
    range_shift,
    angle_shift,
    range_taps,
    angle_taps,
    phase_rates,
    invert,
    baseline_index,
):
    n, passes = mesh_shape["ap"], mesh_shape["pass"]
    pulses, samples = echo.shape[1], echo.shape[3]
    levels = range_taps.shape[0]
    taps_count = chirp.shape[1]
    cells = samples - taps_count
    block = cells // n
    beams = 2**levels
    share = beams // passes
    heights = invert.shape[1]
    count = block * share // LANES
    parts = 2 if count % 16 == 0 else 1
    lanes = n * 2 * pulses
    reach = RMAX + range_taps.shape[2] // 2
    local = pulses.bit_length() - 1
    wide = up(block + 2 * reach * (levels - local), LANES)
    depth = up(block + taps_count - 1, LANES)
    vmem = pl.BlockSpec(memory_space=pltpu.VMEM)
    hbm = pl.BlockSpec(memory_space=pltpu.HBM)
    operands = (
        echo,
        chirp,
        pair_swap,
        jnp.transpose(range_shift, (0, 2, 1)),
        jnp.transpose(angle_shift, (0, 2, 3, 1)),
        range_taps,
        angle_taps,
        jnp.transpose(phase_rates, (1, 2, 3, 0)),
        jnp.transpose(invert, (0, 2, 1)),
        baseline_index,
    )
    held = [
        (pltpu.VMEM if i in (0, 1, 8) else pltpu.SMEM)(operand.shape, operand.dtype)
        for i, operand in enumerate(operands)
    ]
    stacks, mixer = pl.pallas_call(
        functools.partial(image_kernel, (n, passes, pulses, cells, levels)),
        out_shape=(
            jax.ShapeDtypeStruct((parts, passes, 2 * count // parts, LANES), F32),
            jax.ShapeDtypeStruct((2 * heights, 6 * passes), BF16),
        ),
        in_specs=[hbm] * len(operands),
        out_specs=(vmem, vmem),
        scratch_shapes=held
        + [
            pltpu.VMEM((2 * pulses, up(max(samples, block * (n - 1) + depth), LANES)), F32),
            pltpu.VMEM((2 * block, depth), BF16),
            pltpu.VMEM((lanes // LANES, wide + 2 * PAD, LANES), F32),
            pltpu.VMEM((lanes // LANES, wide + 2 * PAD, LANES), F32),
            pltpu.VMEM((lanes // LANES, wide + 8, LANES), F32),
            pltpu.VMEM((wide, 3 * lanes), BF16),
            pltpu.VMEM((max(wide, 2 * block), 4 * lanes), F32),
            pltpu.VMEM((levels, 3 * lanes, 4 * lanes), BF16),
            pltpu.VMEM((levels, 2, 2, 8 + up(wide // 8, 8), lanes), F32),
            pltpu.VMEM((n, 2 * pulses, wide), F32),
            pltpu.VMEM((n, 2 * pulses, wide), F32),
            pltpu.VMEM((parts, passes, 2 * count // parts, LANES), F32),
            pltpu.SemaphoreType.DMA((len(operands),)),
            pltpu.SemaphoreType.DMA((n,)),
            pltpu.SemaphoreType.DMA((n,)),
            pltpu.SemaphoreType.DMA((parts * passes,)),
            pltpu.SemaphoreType.DMA((parts * passes,)),
        ],
        compiler_params=pltpu.CompilerParams(
            collective_id=0,
            has_side_effects=True,
            vmem_limit_bytes=min(56 * 2**20, 16 * 2**20 + 24 * levels * lanes * lanes),
        ),
        name="image",
    )(*[pltpu.with_memory_space_constraint(operand, pltpu.HBM) for operand in operands])
    power = pl.pallas_call(
        functools.partial(power_kernel, passes, parts),
        out_shape=jax.ShapeDtypeStruct((heights, count, LANES), F32),
        in_specs=[vmem, vmem],
        out_specs=hbm,
        scratch_shapes=[
            pltpu.VMEM((heights * (count + 8), LANES), F32),
            pltpu.SemaphoreType.DMA((count,)),
        ],
        compiler_params=pltpu.CompilerParams(vmem_limit_bytes=32 * 2**20),
        name="power",
    )(stacks.reshape(passes * 2 * count, LANES), mixer)
    return power.reshape(1, heights, 1, block * share)


def solution(mesh):
    return jax.shard_map(
        functools.partial(body, dict(mesh.shape)),
        mesh=mesh,
        in_specs=(
            P("pass", "ap", None, None),
            P(),
            P("pass", None),
            P("pass", None, None),
            P("pass", None, None, None),
            P(),
            P(),
            P(),
            P(),
            P(),
        ),
        out_specs=P("pass", None, "ap", None),
        check_vma=False,
    )
```
